256 devices in a mesh: limb: 8 (over y, z_hi), coef: 32 (over z_lo, x, core).
Axes of the slice: x: 4, y: 4, z: 8 (z_hi: 2, z_lo: 4; z = z_hi * 4 + z_lo), core: 2. Of those that a mesh axis runs over, the one named last changes fastest.
Arguments:
- first_cipher: float32 [16, 2, 2, 32768], P('limb', None, None, 'coef'), may hold values from -0.375 to 0.375
- second_cipher: float32 [16, 2, 2, 32768], P('limb', None, None, 'coef'), may hold values from -0.375 to 0.375
- to_special: float32 [16, 16], replicated, may hold values from -1.5 to 1.5
- keep_table: float32 [16, 16], P(None, 'limb'), may hold values from -1 to 1
- scale_table: float32 [16, 16], P(None, 'limb'), may hold values from -1 to 1
Outputs:
- product: float32 [16, 2, 3, 32768], P('limb', None, None, 'coef')
The draws below stay inside these ranges and needn't reach their ends.
All inputs are finite; a program needn't handle non-finite values.
Results may differ from the reference program's by a relative error of at most 0.00012.
Values sent between devices are 32-bit elements; how exact they have to be, the bound alone decides.
No kernel may reach another device: no remote copies, remote signals or barrier semaphores. Data moves between devices by JAX's collectives and lax.ppermute only.
A program may use at most 64 MiB of HBM per device.

```python
import math
import jax
import jax.numpy as jnp
from jax import lax

LQ = 16
LP = 16
N2 = 256
PAIRS = 2
N = 32768


def steps_of(rng, dims, cuts, least, top_value):
    loudness, own = 1.0, jax.random.fold_in(rng, 6)
    for dim, blocks in cuts:
        steps = jnp.exp(jax.random.uniform(jax.random.fold_in(own, dim), (blocks,), jnp.float32, least / len(cuts), top_value / len(cuts)))
        loudness = loudness * jnp.repeat(steps, dims[dim] // blocks).reshape([-1 if axis == dim else 1 for axis in range(len(dims))])
    return loudness


def normal_values(key, extent, deviation, limit, pieces=(), held_as=jnp.bfloat16):
    gain = steps_of(key, extent, pieces, -0.22, 0.18) if pieces else 1.0
    drawn = jax.random.normal(key, extent, jnp.float32) * deviation * gain
    return jnp.minimum(jnp.maximum(drawn, -limit), limit).astype(held_as)


def setup_inputs(seed: int = 0) -> dict:
    seeds = jax.random.split(jax.random.key(seed), 6)
    first_cipher = normal_values(seeds[0], (LQ, PAIRS, 2, N), N2 ** -0.5, 0.375, ((0, 8), (3, 32)), jnp.float32)
    second_cipher = normal_values(seeds[1], (LQ, PAIRS, 2, N), N2 ** -0.5, 0.375, ((0, 8), (3, 32)), jnp.float32)
    to_special = normal_values(seeds[2], (LP, LQ), LQ ** -0.5, 1.5, (), jnp.float32)
    keep_table = normal_values(seeds[3], (LQ, LQ), (LQ + LP) ** -0.5, 1.0, ((1, 8),), jnp.float32)
    scale_table = normal_values(seeds[4], (LQ, LP), (LQ + LP) ** -0.5, 1.0, ((1, 8),), jnp.float32)
    return {"first_cipher": first_cipher, "second_cipher": second_cipher, "to_special": to_special, "keep_table": keep_table, "scale_table": scale_table}


highest = lax.Precision.HIGHEST


def twist_phase(length):
    return jnp.arange(length).astype(jnp.float32) * (math.pi / length)


def spectrum(values):
    phase = twist_phase(values.shape[-1])
    twisted = lax.complex(values * jnp.cos(phase), values * jnp.sin(phase))
    return jnp.fft.fft(twisted, axis=-1)


def restore(spectra):
    phase = twist_phase(spectra.shape[-1])
    signal = jnp.fft.ifft(spectra, axis=-1)
    return jnp.real(signal) * jnp.cos(phase) + jnp.imag(signal) * jnp.sin(phase)


def extend_limbs(to_special, cipher):
    special = jnp.einsum("pq,qcn->pcn", to_special, cipher, precision=highest)
    return jnp.concatenate([cipher, special], axis=0)


def reference(first_cipher, second_cipher, to_special, keep_table, scale_table):
    def pair_tensor(ciphers):
        first_one, second_one = ciphers
        first_freq = spectrum(extend_limbs(to_special, first_one))
        second_freq = spectrum(extend_limbs(to_special, second_one))
        product_low = first_freq[:, 0] * second_freq[:, 0]
        product_mid = first_freq[:, 0] * second_freq[:, 1] + first_freq[:, 1] * second_freq[:, 0]
        product_high = first_freq[:, 1] * second_freq[:, 1]
        return restore(jnp.stack([product_low, product_mid, product_high], axis=1))

    tensor = lax.map(pair_tensor, (jnp.moveaxis(first_cipher, 1, 0), jnp.moveaxis(second_cipher, 1, 0)))
    kept = jnp.einsum("iq,aqcn->iacn", keep_table, tensor[:, :LQ], precision=highest)
    scaled = jnp.einsum("ip,apcn->iacn", scale_table, tensor[:, LQ:], precision=highest)
    return kept + scaled
```

```python
import math

import jax
import jax.numpy as jnp
import ml_dtypes
import numpy as np
from jax import lax
from jax.experimental import pallas as pl
from jax.experimental.pallas import tpu as pltpu
from jax.sharding import PartitionSpec as P

LANES = 128
U = 8
K0 = 8
BLOCK = U * LANES
COEF = 32
GROUPS = 8
ROOTS = 2 * LANES
f32 = jnp.float32
bf16 = jnp.bfloat16


def split_constant(values):
    high = values.astype(np.float32).astype(ml_dtypes.bfloat16)
    low = (values - high.astype(np.float64)).astype(ml_dtypes.bfloat16)
    return high, low


def turn_tables():
    index = np.arange(LANES)
    angle = 2 * np.pi * (index[:, None] * index[None, :] % LANES) / LANES
    wide = np.concatenate([np.cos(angle), np.sin(angle)], axis=1)
    v = np.arange(LANES)[None, :]
    k0 = np.arange(K0)[:, None]
    phase = np.pi * v * (4 * k0 + 1) / 2048
    twiddle = np.concatenate([np.cos(phase), np.sin(phase)], axis=0)
    return split_constant(wide), twiddle.astype(np.float32)


def split_value(values):
    high = values.astype(bf16)
    low = (values - high.astype(f32)).astype(bf16)
    return high, low


def dot3(left, right, dims):
    def one(a, b):
        return lax.dot_general(a, b, (dims, ((), ())), preferred_element_type=f32)

    return one(left[0], right[0]) + (one(left[0], right[1]) + one(left[1], right[0]))


def turn(u, k0):
    angle = math.pi * u * (4 * k0 + 1) / 16
    return math.cos(angle), math.sin(angle)


def evaluate_kernel(first, second, keep, scale, wide_high, wide_low, twiddle, out, held):
    for pair in range(2):
        for u in range(U):
            base = (pair * U + u) * 8
            for limb in range(2):
                for cipher, ref in enumerate((first, second)):
                    held[pl.ds(base + limb * 4 + cipher, 2, stride=2), :] = ref[
                        limb, pair, :, u * LANES : (u + 1) * LANES
                    ]
    rows_real = []
    for pair in range(2):
        parts = [held[(pair * U + u) * 8 : (pair * U + u + 1) * 8, :] for u in range(U)]
        spun = [None] * K0
        for k0 in range(K0 // 2):
            sums = []
            for start in (0, 1):
                real = imag = None
                for u in range(start, U, 2):
                    cosine, sine = turn(u, k0)
                    term_real = parts[u] if u == 0 else parts[u] * cosine
                    real = term_real if real is None else real + term_real
                    if u:
                        term_imag = parts[u] * sine
                        imag = term_imag if imag is None else imag + term_imag
                sums.append((real, imag))
            (even_real, even_imag), (odd_real, odd_imag) = sums
            spun[k0] = (even_real + odd_real, even_imag + odd_imag)
            spun[k0 + K0 // 2] = (even_real - odd_real, even_imag - odd_imag)
        reals, imags = [], []
        for k0 in range(K0):
            cosine = twiddle[k0 : k0 + 1, :]
            sine = twiddle[K0 + k0 : K0 + k0 + 1, :]
            real, imag = spun[k0]
            reals.append(real * cosine - imag * sine)
            imags.append(real * sine + imag * cosine)
        real = jnp.concatenate(reals, axis=0)
        imag = jnp.concatenate(imags, axis=0)
        rows_real.append(jnp.concatenate([real, -imag], axis=1))
        rows_real.append(jnp.concatenate([imag, real], axis=1))
    rows = jnp.concatenate(rows_real, axis=0)
    spectrum = dot3((wide_high[...], wide_low[...]), split_value(rows), ((1,), (1,)))
    lane = lax.broadcasted_iota(jnp.int32, (8, LANES), 1)
    table = jnp.zeros((8, LANES), f32)
    for i in range(16):
        for limb in range(2):
            table = jnp.where(lane == 2 * i + limb, keep[i, limb], table)
            table = jnp.where(lane == 32 + 2 * i + limb, scale[i, limb], table)
    for pair in range(2):
        out[pl.ds(pair * 256, LANES, stride=2), :] = spectrum[:, pair * LANES : (pair + 1) * LANES]
    for tile in range(ROOTS // 8):
        out[pl.ds(tile * 16 + 1, 8, stride=2), :] = table


def complex_scale(value, cosine, sine):
    real, imag = value
    return real * cosine - imag * sine, real * sine + imag * cosine


def split_ring(values, theta):
    if len(values) == 1:
        return [(theta, values[0])]
    half = len(values) // 2
    cosine, sine = math.cos(theta / 2), math.sin(theta / 2)
    left, right = [], []
    for low, high in zip(values[:half], values[half:]):
        moved = complex_scale(high, cosine, sine)
        left.append((low[0] + moved[0], low[1] + moved[1]))
        right.append((low[0] - moved[0], low[1] - moved[1]))
    return split_ring(left, theta / 2) + split_ring(right, theta / 2 + math.pi)


def join_ring(values, theta):
    if len(values) == 1:
        return values
    half = len(values) // 2
    left = join_ring(values[:half], theta / 2)
    right = join_ring(values[half:], theta / 2 + math.pi)
    cosine, sine = math.cos(theta / 2), math.sin(theta / 2)
    low, high = [], []
    for one, two in zip(left, right):
        low.append((one[0] + two[0], one[1] + two[1]))
        high.append(complex_scale((one[0] - two[0], one[1] - two[1]), cosine, -sine))
    return low + high


def root_angles(count, theta):
    if count == 1:
        return [theta]
    return root_angles(count // 2, theta / 2) + root_angles(count // 2, theta / 2 + math.pi)


def tensor_kernel(spread, to_special, out, real_held, imag_held, table_held, table, table_sem):
    table_held[...] = spread[pl.ds(1, GROUPS, stride=2 * COEF), :]
    copy = pltpu.make_async_copy(table_held, table, table_sem)
    copy.start()
    lane = lax.broadcasted_iota(jnp.int32, (8, LANES), 1)
    half = lane < 64
    sign = jnp.where(half, 1.0, -1.0).astype(f32)
    limb_low = (lane & 4) == 0
    comp = lane & 3

    def roll(value, shift):
        return pltpu.roll(value, shift % LANES, 1)

    packed = []
    for e in range(COEF // 2):
        even = spread[pl.ds(4 * e, GROUPS, stride=2 * COEF), :]
        odd = spread[pl.ds(4 * e + 2, GROUPS, stride=2 * COEF), :]
        packed.append((jnp.where(half, even, roll(odd, 64)), jnp.where(half, roll(even, 64), odd)))
    for place, (theta, (real, imag)) in enumerate(split_ring(packed, math.pi)):
        cosine = sign * math.cos(theta / 2)
        sine = sign * math.sin(theta / 2)
        real_other, imag_other = roll(real, 64), roll(imag, 64)
        real_low, imag_low = jnp.where(half, real, real_other), jnp.where(half, imag, imag_other)
        real_high, imag_high = jnp.where(half, real_other, real), jnp.where(half, imag_other, imag)
        real_held[place * 8 : place * 8 + 8, :] = real_low + (cosine * real_high - sine * imag_high)
        imag_held[place * 8 : place * 8 + 8, :] = imag_low + (cosine * imag_high + sine * real_high)

    limbs = []
    for group in range(GROUPS):
        pair = []
        for ref in (real_held, imag_held):
            one = ref[pl.ds(group, 8, stride=8), :]
            two = ref[pl.ds(64 + group, 8, stride=8), :]
            pair.append((jnp.where(limb_low, one, roll(two, 4)), jnp.where(limb_low, roll(one, -4), two)))
        limbs.append((pair[0][0], pair[1][0]))
        limbs.append((pair[0][1], pair[1][1]))

    def tensor(value):
        left, right = [], []
        for part in value:
            after = roll(part, -1)
            left.append(jnp.where(comp == 1, after, jnp.where(comp == 3, roll(part, 3), part)))
            right.append(jnp.where((comp & 1) == 0, after, part))
        return (
            left[0] * right[0] - left[1] * right[1],
            left[0] * right[1] + left[1] * right[0],
        )

    copy.wait()
    totals = [None] * 16
    for q in range(32):
        if q < 16:
            value = limbs[q]
        else:
            real = imag = None
            for s in range(16):
                weight = to_special[q - 16, s]
                term_real, term_imag = weight * limbs[s][0], weight * limbs[s][1]
                real = term_real if real is None else real + term_real
                imag = term_imag if imag is None else imag + term_imag
            value = (real, imag)
        product = tensor(value)
        group, place = (q % 16) // 2, (q % 2) + (0 if q < 16 else 32)
        for i in range(16):
            weight = table[group, place + 2 * i]
            term = (weight * product[0], weight * product[1])
            totals[i] = term if totals[i] is None else (totals[i][0] + term[0], totals[i][1] + term[1])

    for group in range(GROUPS):
        for part, ref in enumerate((real_held, imag_held)):
            low, high = totals[2 * group][part], totals[2 * group + 1][part]
            ref[pl.ds(group, 8, stride=8), :] = jnp.where(limb_low, low, roll(high, 4))
            ref[pl.ds(64 + group, 8, stride=8), :] = jnp.where(limb_low, roll(low, -4), high)

    share = 1.0 / (COEF * BLOCK)
    joined = []
    for place, theta in enumerate(root_angles(COEF // 2, math.pi)):
        real = real_held[place * 8 : place * 8 + 8, :]
        imag = imag_held[place * 8 : place * 8 + 8, :]
        real_other, imag_other = roll(real, 64), roll(imag, 64)
        root = complex(math.cos(theta / 2), math.sin(theta / 2))
        plus, minus = (1 - 1j * root) * share, (1 + 1j * root) * share
        own = (plus, -root.conjugate() * minus)
        other = (minus, root.conjugate() * plus)
        own_real, own_imag = jnp.where(half, own[0].real, own[1].real), jnp.where(half, own[0].imag, own[1].imag)
        other_real = jnp.where(half, other[0].real, other[1].real)
        other_imag = jnp.where(half, other[0].imag, other[1].imag)
        joined.append(
            (
                (own_real * real - own_imag * imag) + (other_real * real_other - other_imag * imag_other),
                (own_real * imag + own_imag * real) + (other_real * imag_other + other_imag * real_other),
            )
        )
    for e, (real, imag) in enumerate(join_ring(joined, math.pi)):
        out[pl.ds(2 * e, GROUPS, stride=COEF), :] = jnp.where(half, real, roll(imag, 64))
        out[pl.ds(2 * e + 1, GROUPS, stride=COEF), :] = jnp.where(half, roll(real, 64), imag)


def restore_kernel(gathered, wide_high, wide_low, twiddle, out):
    row = lax.broadcasted_iota(jnp.int32, (8, LANES), 0)
    middle = (row & 3) == 1
    wide = (wide_high[...], wide_low[...])
    for pair in range(2):
        values = gathered[pair * LANES : (pair + 1) * LANES, :]
        spun = dot3(split_value(values), wide, ((0,), (0,)))
        real = spun[:64, :LANES] + spun[64:, LANES:]
        imag = spun[64:, :LANES] - spun[:64, LANES:]
        turned = []
        for k0 in range(K0):
            cosine = twiddle[k0 : k0 + 1, :]
            sine = twiddle[K0 + k0 : K0 + k0 + 1, :]
            own_real, own_imag = real[k0 * 8 : k0 * 8 + 8], imag[k0 * 8 : k0 * 8 + 8]
            turned.append((own_real * cosine + own_imag * sine, own_imag * cosine - own_real * sine))
        halves = []
        for k0 in range(K0 // 2):
            one, two = turned[k0], turned[k0 + K0 // 2]
            halves.append(((one[0] + two[0], one[1] + two[1]), (one[0] - two[0], one[1] - two[1])))
        for u in range(U):
            total = None
            for k0 in range(K0 // 2):
                cosine, sine = turn(u, k0)
                real_part, imag_part = halves[k0][u % 2]
                term = real_part if u == 0 else real_part * cosine + imag_part * sine
                total = term if total is None else total + term
            total = jnp.where(middle, total + pltpu.roll(total, 6, 0), total)
            for limb in range(2):
                out[limb, pair, :, u * LANES : (u + 1) * LANES] = total[limb * 4 : limb * 4 + 3]


def in_vmem():
    return pl.BlockSpec(memory_space=pltpu.VMEM)


def in_smem():
    return pl.BlockSpec(memory_space=pltpu.SMEM)


def per_device(first_cipher, second_cipher, to_special, keep_table, scale_table):
    (wide_high, wide_low), twiddle = turn_tables()
    wide_high, wide_low, twiddle = jnp.asarray(wide_high), jnp.asarray(wide_low), jnp.asarray(twiddle)
    params = pltpu.CompilerParams(vmem_limit_bytes=32 * 1024 * 1024)
    spectra = pl.pallas_call(
        evaluate_kernel,
        out_shape=jax.ShapeDtypeStruct((2 * ROOTS, LANES), f32),
        in_specs=[in_vmem()] * 2 + [in_smem()] * 2 + [in_vmem()] * 3,
        out_specs=in_vmem(),
        scratch_shapes=[pltpu.VMEM((2 * U * 8, LANES), f32)],
        compiler_params=params,
        name="evaluate",
    )(first_cipher, second_cipher, keep_table, scale_table, wide_high, wide_low, twiddle)
    spread = lax.all_to_all(spectra.reshape(ROOTS, 2, LANES), ("limb", "coef"), 0, 0)
    scaled = pl.pallas_call(
        tensor_kernel,
        out_shape=jax.ShapeDtypeStruct((ROOTS, LANES), f32),
        in_specs=[in_vmem(), in_smem()],
        out_specs=in_vmem(),
        scratch_shapes=[
            pltpu.VMEM((LANES, LANES), f32),
            pltpu.VMEM((LANES, LANES), f32),
            pltpu.VMEM((8, LANES), f32),
            pltpu.SMEM((8, LANES), f32),
            pltpu.SemaphoreType.DMA,
        ],
        compiler_params=params,
        name="tensor",
    )(spread.reshape(2 * ROOTS, LANES), to_special)
    gathered = lax.all_to_all(scaled.reshape(ROOTS, 1, LANES), ("limb", "coef"), 0, 0)
    return pl.pallas_call(
        restore_kernel,
        out_shape=jax.ShapeDtypeStruct((2, 2, 3, BLOCK), f32),
        in_specs=[in_vmem()] * 4,
        out_specs=in_vmem(),
        compiler_params=params,
        name="restore",
    )(gathered.reshape(ROOTS, LANES), wide_high, wide_low, twiddle)


def solution(mesh):
    return jax.shard_map(
        per_device,
        mesh=mesh,
        in_specs=(
            P("limb", None, None, "coef"),
            P("limb", None, None, "coef"),
            P(),
            P(None, "limb"),
            P(None, "limb"),
        ),
        out_specs=P("limb", None, None, "coef"),
        check_vma=False,
    )
```

```python
import math

import jax
import jax.numpy as jnp
import ml_dtypes
import numpy as np
from jax import lax
from jax.experimental import pallas as pl
from jax.experimental.pallas import tpu as pltpu
from jax.sharding import PartitionSpec as P

LANES = 128
U = 8
K0 = 8
BLOCK = U * LANES
COEF = 32
GROUPS = 8
ROOTS = 2 * LANES
f32 = jnp.float32
bf16 = jnp.bfloat16


def split_constant(values):
    high = values.astype(np.float32).astype(ml_dtypes.bfloat16)
    low = (values - high.astype(np.float64)).astype(ml_dtypes.bfloat16)
    return high, low


def turn_tables():
    index = np.arange(LANES)
    angle = 2 * np.pi * (index[:, None] * index[None, :] % LANES) / LANES
    wide = np.concatenate([np.cos(angle), np.sin(angle)], axis=1)
    v = np.arange(LANES)[None, :]
    k0 = np.arange(K0)[:, None]
    phase = np.pi * v * (4 * k0 + 1) / 2048
    twiddle = np.concatenate([np.cos(phase), np.sin(phase)], axis=0)
    return split_constant(wide), twiddle.astype(np.float32)


def split_value(values):
    high = values.astype(bf16)
    low = (values - high.astype(f32)).astype(bf16)
    return high, low


def dot3(left, right, dims):
    def one(a, b):
        return lax.dot_general(a, b, (dims, ((), ())), preferred_element_type=f32)

    return one(left[0], right[0]) + (one(left[0], right[1]) + one(left[1], right[0]))


def turn(u, k0):
    angle = math.pi * u * (4 * k0 + 1) / 16
    return math.cos(angle), math.sin(angle)


def evaluate_kernel(
    first_far, second_far, keep_far, scale_far, high_far, low_far, twiddle_far,
    out,
    first, second, keep, scale, wide_high, wide_low, twiddle, held, sems,
):
    copies = [
        pltpu.make_async_copy(far, near, sems.at[place])
        for place, (far, near) in enumerate(
            (
                (first_far, first),
                (second_far, second),
                (twiddle_far, twiddle),
                (high_far, wide_high),
                (low_far, wide_low),
                (keep_far, keep),
                (scale_far, scale),
            )
        )
    ]
    for copy in copies:
        copy.start()
    copies[0].wait()
    copies[1].wait()
    for pair in range(2):
        for u in range(U):
            base = (pair * U + u) * 8
            for limb in range(2):
                for cipher, ref in enumerate((first, second)):
                    held[pl.ds(base + limb * 4 + cipher, 2, stride=2), :] = ref[
                        limb, pair, :, u * LANES : (u + 1) * LANES
                    ]
    copies[2].wait()
    blocks = []
    for pair in range(2):
        parts = [held[(pair * U + u) * 8 : (pair * U + u + 1) * 8, :] for u in range(U)]
        spun = [None] * K0
        for k0 in range(K0 // 2):
            sums = []
            for start in (0, 1):
                real = imag = None
                for u in range(start, U, 2):
                    cosine, sine = turn(u, k0)
                    term_real = parts[u] if u == 0 else parts[u] * cosine
                    real = term_real if real is None else real + term_real
                    if u:
                        term_imag = parts[u] * sine
                        imag = term_imag if imag is None else imag + term_imag
                sums.append((real, imag))
            (even_real, even_imag), (odd_real, odd_imag) = sums
            spun[k0] = (even_real + odd_real, even_imag + odd_imag)
            spun[k0 + K0 // 2] = (even_real - odd_real, even_imag - odd_imag)
        reals, imags = [], []
        for k0 in range(K0):
            cosine = twiddle[k0 : k0 + 1, :]
            sine = twiddle[K0 + k0 : K0 + k0 + 1, :]
            real, imag = spun[k0]
            reals.append(real * cosine - imag * sine)
            imags.append(real * sine + imag * cosine)
        real = jnp.concatenate(reals, axis=0)
        imag = jnp.concatenate(imags, axis=0)
        blocks.append(jnp.concatenate([real, -imag], axis=1))
        blocks.append(jnp.concatenate([imag, real], axis=1))
    rows = jnp.concatenate(blocks, axis=0)
    copies[3].wait()
    copies[4].wait()
    spectrum = dot3((wide_high[...], wide_low[...]), split_value(rows), ((1,), (1,)))
    copies[5].wait()
    copies[6].wait()
    lane = lax.broadcasted_iota(jnp.int32, (8, LANES), 1)
    table = jnp.zeros((8, LANES), f32)
    for i in range(16):
        for limb in range(2):
            place = limb * 16 + (i % 2) * 8 + i // 2
            table = jnp.where(lane == place, keep[limb, i], table)
            table = jnp.where(lane == 32 + place, scale[limb, i], table)
    for pair in range(2):
        out[pl.ds(pair * 256, LANES, stride=2), :] = spectrum[:, pair * LANES : (pair + 1) * LANES]
    for tile in range(ROOTS // 8):
        out[pl.ds(tile * 16 + 1, 8, stride=2), :] = table


def complex_scale(value, cosine, sine):
    real, imag = value
    return real * cosine - imag * sine, real * sine + imag * cosine


def split_ring(values, theta):
    if len(values) == 1:
        return [(theta, values[0])]
    half = len(values) // 2
    cosine, sine = math.cos(theta / 2), math.sin(theta / 2)
    left, right = [], []
    for low, high in zip(values[:half], values[half:]):
        moved = complex_scale(high, cosine, sine)
        left.append((low[0] + moved[0], low[1] + moved[1]))
        right.append((low[0] - moved[0], low[1] - moved[1]))
    return split_ring(left, theta / 2) + split_ring(right, theta / 2 + math.pi)


def join_ring(values, theta):
    if len(values) == 1:
        return values
    half = len(values) // 2
    left = join_ring(values[:half], theta / 2)
    right = join_ring(values[half:], theta / 2 + math.pi)
    cosine, sine = math.cos(theta / 2), math.sin(theta / 2)
    low, high = [], []
    for one, two in zip(left, right):
        low.append((one[0] + two[0], one[1] + two[1]))
        high.append(complex_scale((one[0] - two[0], one[1] - two[1]), cosine, -sine))
    return low + high


def root_angles(count, theta):
    if count == 1:
        return [theta]
    return root_angles(count // 2, theta / 2) + root_angles(count // 2, theta / 2 + math.pi)


def mix(weights, values, dims):
    high, low = split_value(values)
    axis = dims[0][0]
    left = jnp.concatenate([weights[0], weights[0], weights[1]], axis=axis)
    return lax.dot_general(
        left, jnp.concatenate([high, low, high], axis=0), (dims, ((), ())), preferred_element_type=f32
    )


def tensor_kernel(spread, to_special, out):
    lane = lax.broadcasted_iota(jnp.int32, (8, LANES), 1)
    half = lane < 64
    sign = jnp.where(half, 1.0, -1.0).astype(f32)
    limb_low = (lane & 4) == 0
    comp = lax.broadcasted_iota(jnp.int32, (16, LANES), 1) & 3

    def roll(value, shift):
        return pltpu.roll(value, shift % LANES, 1)

    rows = jnp.concatenate([to_special[pl.ds(limb, 8, stride=2), :] for limb in range(2)], axis=0)
    old = lax.broadcasted_iota(jnp.int32, (16, 16), 0)
    new = lax.broadcasted_iota(jnp.int32, (16, 16), 1)
    order = jnp.where(old == 2 * (new & 7) + (new >> 3), 1.0, 0.0).astype(bf16)
    extend = split_value(
        sum(
            lax.dot_general(part, order, (((1,), (0,)), ((), ())), preferred_element_type=f32)
            for part in split_value(rows)
        )
    )
    table = spread[pl.ds(1, GROUPS, stride=2 * COEF), :]
    shrink = split_value(jnp.concatenate([table[:, 16 * j : 16 * j + 16] for j in range(4)], axis=0))

    packed = []
    for e in range(COEF // 2):
        even = spread[pl.ds(4 * e, GROUPS, stride=2 * COEF), :]
        odd = spread[pl.ds(4 * e + 2, GROUPS, stride=2 * COEF), :]
        packed.append((jnp.where(half, even, roll(odd, 64)), jnp.where(half, roll(even, 64), odd)))
    spectra = []
    for theta, (real, imag) in split_ring(packed, math.pi):
        cosine = sign * math.cos(theta / 2)
        sine = sign * math.sin(theta / 2)
        real_other, imag_other = roll(real, 64), roll(imag, 64)
        real_low, imag_low = jnp.where(half, real, real_other), jnp.where(half, imag, imag_other)
        real_high, imag_high = jnp.where(half, real_other, real), jnp.where(half, imag_other, imag)
        spectra.append(
            (
                real_low + (cosine * real_high - sine * imag_high),
                imag_low + (cosine * imag_high + sine * real_high),
            )
        )

    def tensor(value):
        left, right = [], []
        for part in value:
            after = roll(part, -1)
            left.append(jnp.where(comp == 1, after, jnp.where(comp == 3, roll(part, 3), part)))
            right.append(jnp.where((comp & 1) == 0, after, part))
        return (
            left[0] * right[0] - left[1] * right[1],
            left[0] * right[1] + left[1] * right[0],
        )

    mixed = []
    for place in range(COEF // 4):
        own = []
        for part in range(2):
            one, two = spectra[2 * place][part], spectra[2 * place + 1][part]
            own.append(
                jnp.concatenate(
                    [jnp.where(limb_low, one, roll(two, 4)), jnp.where(limb_low, roll(one, -4), two)], axis=0
                )
            )
        special = mix(extend, jnp.concatenate(own, axis=1), ((1,), (0,)))
        own = tensor(own)
        special = tensor((special[:, :LANES], special[:, LANES:]))
        products = jnp.concatenate(
            [jnp.concatenate(own, axis=1), jnp.concatenate(special, axis=1)], axis=0
        )
        scaled = mix(shrink, products, ((0,), (0,)))
        parts = []
        for part in range(2):
            both = scaled[:, part * LANES : (part + 1) * LANES]
            low, high = both[:8], both[8:]
            parts.append((jnp.where(limb_low, low, roll(high, 4)), jnp.where(limb_low, roll(low, -4), high)))
        mixed.append((parts[0][0], parts[1][0]))
        mixed.append((parts[0][1], parts[1][1]))

    share = 1.0 / (COEF * BLOCK)
    joined = []
    for (real, imag), theta in zip(mixed, root_angles(COEF // 2, math.pi)):
        real_other, imag_other = roll(real, 64), roll(imag, 64)
        root = complex(math.cos(theta / 2), math.sin(theta / 2))
        plus, minus = (1 - 1j * root) * share, (1 + 1j * root) * share
        own = (plus, -root.conjugate() * minus)
        other = (minus, root.conjugate() * plus)
        own_real, own_imag = jnp.where(half, own[0].real, own[1].real), jnp.where(half, own[0].imag, own[1].imag)
        other_real = jnp.where(half, other[0].real, other[1].real)
        other_imag = jnp.where(half, other[0].imag, other[1].imag)
        joined.append(
            (
                (own_real * real - own_imag * imag) + (other_real * real_other - other_imag * imag_other),
                (own_real * imag + own_imag * real) + (other_real * imag_other + other_imag * real_other),
            )
        )
    for e, (real, imag) in enumerate(join_ring(joined, math.pi)):
        out[pl.ds(2 * e, GROUPS, stride=COEF), :] = jnp.where(half, real, roll(imag, 64))
        out[pl.ds(2 * e + 1, GROUPS, stride=COEF), :] = jnp.where(half, roll(real, 64), imag)


def restore_kernel(gathered, wide_high, wide_low, twiddle, out):
    row = lax.broadcasted_iota(jnp.int32, (8, LANES), 0)
    middle = (row & 3) == 1
    wide = (wide_high[...], wide_low[...])
    for pair in range(2):
        values = gathered[pair * LANES : (pair + 1) * LANES, :]
        spun = dot3(split_value(values), wide, ((0,), (0,)))
        real = spun[:64, :LANES] + spun[64:, LANES:]
        imag = spun[64:, :LANES] - spun[:64, LANES:]
        turned = []
        for k0 in range(K0):
            cosine = twiddle[k0 : k0 + 1, :]
            sine = twiddle[K0 + k0 : K0 + k0 + 1, :]
            own_real, own_imag = real[k0 * 8 : k0 * 8 + 8], imag[k0 * 8 : k0 * 8 + 8]
            turned.append((own_real * cosine + own_imag * sine, own_imag * cosine - own_real * sine))
        halves = []
        for k0 in range(K0 // 2):
            one, two = turned[k0], turned[k0 + K0 // 2]
            halves.append(((one[0] + two[0], one[1] + two[1]), (one[0] - two[0], one[1] - two[1])))
        for u in range(U):
            total = None
            for k0 in range(K0 // 2):
                cosine, sine = turn(u, k0)
                real_part, imag_part = halves[k0][u % 2]
                term = real_part if u == 0 else real_part * cosine + imag_part * sine
                total = term if total is None else total + term
            total = jnp.where(middle, total + pltpu.roll(total, 6, 0), total)
            for limb in range(2):
                for part in range(3):
                    row = limb * 4 + part
                    out[limb, part, pair : pair + 1, u * LANES : (u + 1) * LANES] = total[row : row + 1]


def in_vmem():
    return pl.BlockSpec(memory_space=pltpu.VMEM)


def in_hbm():
    return pl.BlockSpec(memory_space=pltpu.HBM)


def kept_far(*arrays):
    return [pltpu.with_memory_space_constraint(array, pltpu.HBM) for array in arrays]


def per_device(first_cipher, second_cipher, to_special, keep_table, scale_table):
    (wide_high, wide_low), twiddle = turn_tables()
    wide_high, wide_low, twiddle = jnp.asarray(wide_high), jnp.asarray(wide_low), jnp.asarray(twiddle)
    params = pltpu.CompilerParams(vmem_limit_bytes=32 * 1024 * 1024)
    spectra = pl.pallas_call(
        evaluate_kernel,
        out_shape=jax.ShapeDtypeStruct((2 * ROOTS, LANES), f32),
        in_specs=[in_hbm()] * 7,
        out_specs=in_vmem(),
        scratch_shapes=[
            pltpu.VMEM(first_cipher.shape, f32),
            pltpu.VMEM(second_cipher.shape, f32),
            pltpu.SMEM((2, 16), f32),
            pltpu.SMEM((2, 16), f32),
            pltpu.VMEM(wide_high.shape, bf16),
            pltpu.VMEM(wide_low.shape, bf16),
            pltpu.VMEM(twiddle.shape, f32),
            pltpu.VMEM((2 * U * 8, LANES), f32),
            pltpu.SemaphoreType.DMA((7,)),
        ],
        compiler_params=params,
        name="evaluate",
    )(*kept_far(first_cipher, second_cipher, keep_table.T, scale_table.T, wide_high, wide_low, twiddle))
    spread = lax.all_to_all(spectra.reshape(ROOTS, 2, LANES), ("limb", "coef"), 0, 0)
    scaled = pl.pallas_call(
        tensor_kernel,
        out_shape=jax.ShapeDtypeStruct((ROOTS, LANES), f32),
        in_specs=[in_vmem()] * 2,
        out_specs=in_vmem(),
        compiler_params=params,
        name="tensor",
    )(spread.reshape(2 * ROOTS, LANES), to_special)
    gathered = lax.all_to_all(scaled.reshape(ROOTS, 1, LANES), ("limb", "coef"), 0, 0)
    product = pl.pallas_call(
        restore_kernel,
        out_shape=jax.ShapeDtypeStruct((2, 3, 2, BLOCK), f32),
        in_specs=[in_vmem()] * 4,
        out_specs=in_vmem(),
        compiler_params=params,
        name="restore",
    )(gathered.reshape(ROOTS, LANES), wide_high, wide_low, twiddle)
    return product.transpose(0, 2, 1, 3)


def solution(mesh):
    return jax.shard_map(
        per_device,
        mesh=mesh,
        in_specs=(
            P("limb", None, None, "coef"),
            P("limb", None, None, "coef"),
            P(),
            P(None, "limb"),
            P(None, "limb"),
        ),
        out_specs=P("limb", None, None, "coef"),
        check_vma=False,
    )
```

```python
import math

import jax
import jax.numpy as jnp
import ml_dtypes
import numpy as np
from jax import lax
from jax.experimental import pallas as pl
from jax.experimental.pallas import tpu as pltpu
from jax.sharding import PartitionSpec as P

LANES = 128
U = 8
K0 = 8
BLOCK = U * LANES
COEF = 32
GROUPS = 8
ROOTS = 2 * LANES
f32 = jnp.float32
bf16 = jnp.bfloat16


def split_constant(values):
    high = values.astype(np.float32).astype(ml_dtypes.bfloat16)
    low = (values - high.astype(np.float64)).astype(ml_dtypes.bfloat16)
    return high, low


def turn_tables():
    index = np.arange(LANES)
    angle = 2 * np.pi * (index[:, None] * index[None, :] % LANES) / LANES
    wide = np.concatenate([np.cos(angle), np.sin(angle)], axis=1)
    v = np.arange(LANES)[None, :]
    k0 = np.arange(K0)[:, None]
    phase = np.pi * v * (4 * k0 + 1) / 2048
    twiddle = np.concatenate([np.cos(phase), np.sin(phase)], axis=0)
    return split_constant(wide), twiddle.astype(np.float32)


def split_value(values):
    high = values.astype(bf16)
    low = (values - high.astype(f32)).astype(bf16)
    return high, low


def dot3(left, right, dims):
    def one(a, b):
        return lax.dot_general(a, b, (dims, ((), ())), preferred_element_type=f32)

    return one(left[0], right[0]) + (one(left[0], right[1]) + one(left[1], right[0]))


def turn(u, k0):
    angle = math.pi * u * (4 * k0 + 1) / 16
    return math.cos(angle), math.sin(angle)


def evaluate_kernel(
    first_far, second_far, keep_far, scale_far, high_far, low_far, twiddle_far,
    out,
    first, second, keep, scale, wide_high, wide_low, twiddle, held, sems,
):
    copies = [
        pltpu.make_async_copy(far, near, sems.at[place])
        for place, (far, near) in enumerate(
            (
                (first_far, first),
                (second_far, second),
                (twiddle_far, twiddle),
                (high_far, wide_high),
                (low_far, wide_low),
                (keep_far, keep),
                (scale_far, scale),
            )
        )
    ]
    for copy in copies:
        copy.start()
    copies[0].wait()
    copies[1].wait()
    for pair in range(2):
        for u in range(U):
            base = (pair * U + u) * 8
            for limb in range(2):
                for cipher, ref in enumerate((first, second)):
                    held[pl.ds(base + limb * 4 + cipher, 2, stride=2), :] = ref[
                        limb, pair, :, u * LANES : (u + 1) * LANES
                    ]
    copies[2].wait()
    blocks = []
    for pair in range(2):
        parts = [held[(pair * U + u) * 8 : (pair * U + u + 1) * 8, :] for u in range(U)]
        spun = [None] * K0
        for k0 in range(K0 // 2):
            sums = []
            for start in (0, 1):
                real = imag = None
                for u in range(start, U, 2):
                    cosine, sine = turn(u, k0)
                    term_real = parts[u] if u == 0 else parts[u] * cosine
                    real = term_real if real is None else real + term_real
                    if u:
                        term_imag = parts[u] * sine
                        imag = term_imag if imag is None else imag + term_imag
                sums.append((real, imag))
            (even_real, even_imag), (odd_real, odd_imag) = sums
            spun[k0] = (even_real + odd_real, even_imag + odd_imag)
            spun[k0 + K0 // 2] = (even_real - odd_real, even_imag - odd_imag)
        reals, imags = [], []
        for k0 in range(K0):
            cosine = twiddle[k0 : k0 + 1, :]
            sine = twiddle[K0 + k0 : K0 + k0 + 1, :]
            real, imag = spun[k0]
            reals.append(real * cosine - imag * sine)
            imags.append(real * sine + imag * cosine)
        real = jnp.concatenate(reals, axis=0)
        imag = jnp.concatenate(imags, axis=0)
        blocks.append(jnp.concatenate([real, -imag], axis=1))
        blocks.append(jnp.concatenate([imag, real], axis=1))
    rows = jnp.concatenate(blocks, axis=0)
    copies[3].wait()
    copies[4].wait()
    spectrum = dot3((wide_high[...], wide_low[...]), split_value(rows), ((1,), (1,)))
    copies[5].wait()
    copies[6].wait()
    lane = lax.broadcasted_iota(jnp.int32, (8, LANES), 1)
    table = jnp.zeros((8, LANES), f32)
    for i in range(16):
        for limb in range(2):
            place = limb * 16 + (i % 2) * 8 + i // 2
            table = jnp.where(lane == place, keep[limb, i], table)
            table = jnp.where(lane == 32 + place, scale[limb, i], table)
    for pair in range(2):
        out[pl.ds(pair * 256, LANES, stride=2), :] = spectrum[:, pair * LANES : (pair + 1) * LANES]
    for tile in range(ROOTS // 8):
        out[pl.ds(tile * 16 + 1, 8, stride=2), :] = table


def complex_scale(value, cosine, sine):
    real, imag = value
    return real * cosine - imag * sine, real * sine + imag * cosine


def split_ring(values, theta):
    if len(values) == 1:
        return [(theta, values[0])]
    half = len(values) // 2
    cosine, sine = math.cos(theta / 2), math.sin(theta / 2)
    left, right = [], []
    for low, high in zip(values[:half], values[half:]):
        moved = complex_scale(high, cosine, sine)
        left.append((low[0] + moved[0], low[1] + moved[1]))
        right.append((low[0] - moved[0], low[1] - moved[1]))
    return split_ring(left, theta / 2) + split_ring(right, theta / 2 + math.pi)


def join_ring(values, theta):
    if len(values) == 1:
        return values
    half = len(values) // 2
    left = join_ring(values[:half], theta / 2)
    right = join_ring(values[half:], theta / 2 + math.pi)
    cosine, sine = math.cos(theta / 2), math.sin(theta / 2)
    low, high = [], []
    for one, two in zip(left, right):
        low.append((one[0] + two[0], one[1] + two[1]))
        high.append(complex_scale((one[0] - two[0], one[1] - two[1]), cosine, -sine))
    return low + high


def root_angles(count, theta):
    if count == 1:
        return [theta]
    return root_angles(count // 2, theta / 2) + root_angles(count // 2, theta / 2 + math.pi)


def mix(weights, values, dims):
    high, low = split_value(values)
    axis = dims[0][0]
    left = jnp.concatenate([weights[0], weights[0], weights[1]], axis=axis)
    return lax.dot_general(
        left, jnp.concatenate([high, low, high], axis=0), (dims, ((), ())), preferred_element_type=f32
    )


def tensor_kernel(spread, to_special, out):
    lane = lax.broadcasted_iota(jnp.int32, (8, LANES), 1)
    half = lane < 64
    sign = jnp.where(half, 1.0, -1.0).astype(f32)
    limb_low = (lane & 4) == 0
    comp = lax.broadcasted_iota(jnp.int32, (16, LANES), 1) & 3

    def roll(value, shift):
        return pltpu.roll(value, shift % LANES, 1)

    rows = jnp.concatenate([to_special[pl.ds(limb, 8, stride=2), :] for limb in range(2)], axis=0)
    old = lax.broadcasted_iota(jnp.int32, (16, 16), 0)
    new = lax.broadcasted_iota(jnp.int32, (16, 16), 1)
    order = jnp.where(old == 2 * (new & 7) + (new >> 3), 1.0, 0.0).astype(bf16)
    extend = split_value(
        sum(
            lax.dot_general(part, order, (((1,), (0,)), ((), ())), preferred_element_type=f32)
            for part in split_value(rows)
        )
    )
    table = spread[pl.ds(1, GROUPS, stride=2 * COEF), :]
    shrink = split_value(jnp.concatenate([table[:, 16 * j : 16 * j + 16] for j in range(4)], axis=0))

    packed = []
    for e in range(COEF // 2):
        even = spread[pl.ds(4 * e, GROUPS, stride=2 * COEF), :]
        odd = spread[pl.ds(4 * e + 2, GROUPS, stride=2 * COEF), :]
        packed.append((jnp.where(half, even, roll(odd, 64)), jnp.where(half, roll(even, 64), odd)))
    spectra = []
    for theta, (real, imag) in split_ring(packed, math.pi):
        cosine = sign * math.cos(theta / 2)
        sine = sign * math.sin(theta / 2)
        real_other, imag_other = roll(real, 64), roll(imag, 64)
        real_low, imag_low = jnp.where(half, real, real_other), jnp.where(half, imag, imag_other)
        real_high, imag_high = jnp.where(half, real_other, real), jnp.where(half, imag_other, imag)
        spectra.append(
            (
                real_low + (cosine * real_high - sine * imag_high),
                imag_low + (cosine * imag_high + sine * real_high),
            )
        )

    def tensor(value):
        left, right = [], []
        for part in value:
            after = roll(part, -1)
            left.append(jnp.where(comp == 1, after, jnp.where(comp == 3, roll(part, 3), part)))
            right.append(jnp.where((comp & 1) == 0, after, part))
        return (
            left[0] * right[0] - left[1] * right[1],
            left[0] * right[1] + left[1] * right[0],
        )

    owns = []
    for place in range(COEF // 4):
        for part in range(2):
            one, two = spectra[2 * place][part], spectra[2 * place + 1][part]
            owns.append(
                jnp.concatenate(
                    [jnp.where(limb_low, one, roll(two, 4)), jnp.where(limb_low, roll(one, -4), two)], axis=0
                )
            )
    specials = mix(extend, jnp.concatenate(owns, axis=1), ((1,), (0,)))
    own_products, special_products = [], []
    for place in range(COEF // 4):
        start = place * 2 * LANES
        own_products += tensor(owns[2 * place : 2 * place + 2])
        special_products += tensor(
            (specials[:, start : start + LANES], specials[:, start + LANES : start + 2 * LANES])
        )
    products = jnp.concatenate(
        [jnp.concatenate(own_products, axis=1), jnp.concatenate(special_products, axis=1)], axis=0
    )
    scaled = mix(shrink, products, ((0,), (0,)))
    mixed = []
    for place in range(COEF // 4):
        parts = []
        for part in range(2):
            start = (2 * place + part) * LANES
            low, high = scaled[:8, start : start + LANES], scaled[8:, start : start + LANES]
            parts.append((jnp.where(limb_low, low, roll(high, 4)), jnp.where(limb_low, roll(low, -4), high)))
        mixed.append((parts[0][0], parts[1][0]))
        mixed.append((parts[0][1], parts[1][1]))

    share = 1.0 / (COEF * BLOCK)
    joined = []
    for (real, imag), theta in zip(mixed, root_angles(COEF // 2, math.pi)):
        real_other, imag_other = roll(real, 64), roll(imag, 64)
        root = complex(math.cos(theta / 2), math.sin(theta / 2))
        plus, minus = (1 - 1j * root) * share, (1 + 1j * root) * share
        own = (plus, -root.conjugate() * minus)
        other = (minus, root.conjugate() * plus)
        own_real, own_imag = jnp.where(half, own[0].real, own[1].real), jnp.where(half, own[0].imag, own[1].imag)
        other_real = jnp.where(half, other[0].real, other[1].real)
        other_imag = jnp.where(half, other[0].imag, other[1].imag)
        joined.append(
            (
                (own_real * real - own_imag * imag) + (other_real * real_other - other_imag * imag_other),
                (own_real * imag + own_imag * real) + (other_real * imag_other + other_imag * real_other),
            )
        )
    for e, (real, imag) in enumerate(join_ring(joined, math.pi)):
        out[pl.ds(2 * e, GROUPS, stride=COEF), :] = jnp.where(half, real, roll(imag, 64))
        out[pl.ds(2 * e + 1, GROUPS, stride=COEF), :] = jnp.where(half, roll(real, 64), imag)


def restore_kernel(gathered, wide_high, wide_low, twiddle, out):
    row = lax.broadcasted_iota(jnp.int32, (8, LANES), 0)
    middle = (row & 3) == 1
    wide = (wide_high[...], wide_low[...])
    for pair in range(2):
        values = gathered[pair * LANES : (pair + 1) * LANES, :]
        spun = dot3(split_value(values), wide, ((0,), (0,)))
        real = spun[:64, :LANES] + spun[64:, LANES:]
        imag = spun[64:, :LANES] - spun[:64, LANES:]
        turned = []
        for k0 in range(K0):
            cosine = twiddle[k0 : k0 + 1, :]
            sine = twiddle[K0 + k0 : K0 + k0 + 1, :]
            own_real, own_imag = real[k0 * 8 : k0 * 8 + 8], imag[k0 * 8 : k0 * 8 + 8]
            turned.append((own_real * cosine + own_imag * sine, own_imag * cosine - own_real * sine))
        halves = []
        for k0 in range(K0 // 2):
            one, two = turned[k0], turned[k0 + K0 // 2]
            halves.append(((one[0] + two[0], one[1] + two[1]), (one[0] - two[0], one[1] - two[1])))
        for u in range(U):
            total = None
            for k0 in range(K0 // 2):
                cosine, sine = turn(u, k0)
                real_part, imag_part = halves[k0][u % 2]
                term = real_part if u == 0 else real_part * cosine + imag_part * sine
                total = term if total is None else total + term
            total = jnp.where(middle, total + pltpu.roll(total, 6, 0), total)
            for limb in range(2):
                for part in range(3):
                    row = limb * 4 + part
                    out[limb, part, pair : pair + 1, u * LANES : (u + 1) * LANES] = total[row : row + 1]


def in_vmem():
    return pl.BlockSpec(memory_space=pltpu.VMEM)


def in_hbm():
    return pl.BlockSpec(memory_space=pltpu.HBM)


def kept_far(*arrays):
    return [pltpu.with_memory_space_constraint(array, pltpu.HBM) for array in arrays]


def per_device(first_cipher, second_cipher, to_special, keep_table, scale_table):
    (wide_high, wide_low), twiddle = turn_tables()
    wide_high, wide_low, twiddle = jnp.asarray(wide_high), jnp.asarray(wide_low), jnp.asarray(twiddle)
    params = pltpu.CompilerParams(vmem_limit_bytes=32 * 1024 * 1024)
    spectra = pl.pallas_call(
        evaluate_kernel,
        out_shape=jax.ShapeDtypeStruct((2 * ROOTS, LANES), f32),
        in_specs=[in_hbm()] * 7,
        out_specs=in_vmem(),
        scratch_shapes=[
            pltpu.VMEM(first_cipher.shape, f32),
            pltpu.VMEM(second_cipher.shape, f32),
            pltpu.SMEM((2, 16), f32),
            pltpu.SMEM((2, 16), f32),
            pltpu.VMEM(wide_high.shape, bf16),
            pltpu.VMEM(wide_low.shape, bf16),
            pltpu.VMEM(twiddle.shape, f32),
            pltpu.VMEM((2 * U * 8, LANES), f32),
            pltpu.SemaphoreType.DMA((7,)),
        ],
        compiler_params=params,
        name="evaluate",
    )(*kept_far(first_cipher, second_cipher, keep_table.T, scale_table.T, wide_high, wide_low, twiddle))
    spread = lax.all_to_all(spectra.reshape(ROOTS, 2, LANES), ("limb", "coef"), 0, 0)
    scaled = pl.pallas_call(
        tensor_kernel,
        out_shape=jax.ShapeDtypeStruct((ROOTS, LANES), f32),
        in_specs=[in_vmem()] * 2,
        out_specs=in_vmem(),
        compiler_params=params,
        name="tensor",
    )(spread.reshape(2 * ROOTS, LANES), to_special)
    gathered = lax.all_to_all(scaled.reshape(ROOTS, 1, LANES), ("limb", "coef"), 0, 0)
    product = pl.pallas_call(
        restore_kernel,
        out_shape=jax.ShapeDtypeStruct((2, 3, 2, BLOCK), f32),
        in_specs=[in_vmem()] * 4,
        out_specs=in_vmem(),
        compiler_params=params,
        name="restore",
    )(gathered.reshape(ROOTS, LANES), wide_high, wide_low, twiddle)
    return product.transpose(0, 2, 1, 3)


def solution(mesh):
    return jax.shard_map(
        per_device,
        mesh=mesh,
        in_specs=(
            P("limb", None, None, "coef"),
            P("limb", None, None, "coef"),
            P(),
            P(None, "limb"),
            P(None, "limb"),
        ),
        out_specs=P("limb", None, None, "coef"),
        check_vma=False,
    )
```

```python
import math

import jax
import jax.numpy as jnp
import ml_dtypes
import numpy as np
from jax import lax
from jax.experimental import pallas as pl
from jax.experimental.pallas import tpu as pltpu
from jax.sharding import PartitionSpec as P

LANES = 128
U = 8
K0 = 8
BLOCK = U * LANES
COEF = 32
GROUPS = 8
ROOTS = 2 * LANES
f32 = jnp.float32
bf16 = jnp.bfloat16


def split_constant(values):
    high = values.astype(np.float32).astype(ml_dtypes.bfloat16)
    low = (values - high.astype(np.float64)).astype(ml_dtypes.bfloat16)
    return high, low


def turn_tables():
    index = np.arange(LANES)
    angle = 2 * np.pi * (index[:, None] * index[None, :] % LANES) / LANES
    wide = np.concatenate([np.cos(angle), np.sin(angle)], axis=1)
    v = np.arange(LANES)[None, :]
    k0 = np.arange(K0)[:, None]
    phase = np.pi * v * (4 * k0 + 1) / 2048
    twiddle = np.concatenate([np.cos(phase), np.sin(phase)], axis=0)
    return split_constant(wide), twiddle.astype(np.float32)


def split_value(values):
    high = values.astype(bf16)
    low = (values - high.astype(f32)).astype(bf16)
    return high, low


def dot3(left, right, dims):
    def one(a, b):
        return lax.dot_general(a, b, (dims, ((), ())), preferred_element_type=f32)

    return one(left[0], right[0]) + (one(left[0], right[1]) + one(left[1], right[0]))


def turn(u, k0):
    angle = math.pi * u * (4 * k0 + 1) / 16
    return math.cos(angle), math.sin(angle)


def evaluate_kernel(
    first_far, second_far, keep_far, scale_far, high_far, low_far, twiddle_far,
    out,
    first, second, keep, scale, wide_high, wide_low, twiddle, held, sems,
):
    copies = [
        pltpu.make_async_copy(far, near, sems.at[place])
        for place, (far, near) in enumerate(
            (
                (first_far, first),
                (second_far, second),
                (twiddle_far, twiddle),
                (high_far, wide_high),
                (low_far, wide_low),
                (keep_far, keep),
                (scale_far, scale),
            )
        )
    ]
    for copy in copies:
        copy.start()
    copies[0].wait()
    copies[1].wait()
    for pair in range(2):
        for u in range(U):
            base = (pair * U + u) * 8
            for limb in range(2):
                for cipher, ref in enumerate((first, second)):
                    held[pl.ds(base + limb * 4 + cipher, 2, stride=2), :] = ref[
                        limb, pair, :, u * LANES : (u + 1) * LANES
                    ]
    copies[2].wait()
    blocks = []
    for pair in range(2):
        parts = [held[(pair * U + u) * 8 : (pair * U + u + 1) * 8, :] for u in range(U)]
        spun = [None] * K0
        for k0 in range(K0 // 2):
            sums = []
            for start in (0, 1):
                real = imag = None
                for u in range(start, U, 2):
                    cosine, sine = turn(u, k0)
                    term_real = parts[u] if u == 0 else parts[u] * cosine
                    real = term_real if real is None else real + term_real
                    if u:
                        term_imag = parts[u] * sine
                        imag = term_imag if imag is None else imag + term_imag
                sums.append((real, imag))
            (even_real, even_imag), (odd_real, odd_imag) = sums
            spun[k0] = (even_real + odd_real, even_imag + odd_imag)
            spun[k0 + K0 // 2] = (even_real - odd_real, even_imag - odd_imag)
        reals, imags = [], []
        for k0 in range(K0):
            cosine = twiddle[k0 : k0 + 1, :]
            sine = twiddle[K0 + k0 : K0 + k0 + 1, :]
            real, imag = spun[k0]
            reals.append(real * cosine - imag * sine)
            imags.append(real * sine + imag * cosine)
        real = jnp.concatenate(reals, axis=0)
        imag = jnp.concatenate(imags, axis=0)
        blocks.append(jnp.concatenate([real, -imag], axis=1))
        blocks.append(jnp.concatenate([imag, real], axis=1))
    rows = jnp.concatenate(blocks, axis=0)
    copies[3].wait()
    copies[4].wait()
    parted = split_value(rows)
    spectrum = lax.dot_general(
        jnp.concatenate([wide_high[...], wide_high[...], wide_low[...]], axis=1),
        jnp.concatenate([parted[0], parted[1], parted[0]], axis=1),
        (((1,), (1,)), ((), ())),
        preferred_element_type=f32,
    )
    copies[5].wait()
    copies[6].wait()
    lane = lax.broadcasted_iota(jnp.int32, (8, LANES), 1)
    table = jnp.zeros((8, LANES), f32)
    for i in range(16):
        for limb in range(2):
            place = limb * 16 + (i % 2) * 8 + i // 2
            table = jnp.where(lane == place, keep[limb, i], table)
            table = jnp.where(lane == 32 + place, scale[limb, i], table)
    for pair in range(2):
        out[pl.ds(pair * 256, LANES, stride=2), :] = spectrum[:, pair * LANES : (pair + 1) * LANES]
    for tile in range(ROOTS // 8):
        out[pl.ds(tile * 16 + 1, 8, stride=2), :] = table


def complex_scale(value, cosine, sine):
    real, imag = value
    if abs(cosine) < 1e-9:
        return (-imag, real) if sine > 0 else (imag, -real)
    if abs(abs(cosine) - abs(sine)) < 1e-9:
        if cosine * sine > 0:
            return (real - imag) * cosine, (real + imag) * cosine
        return (real + imag) * cosine, (imag - real) * cosine
    return real * cosine - imag * sine, real * sine + imag * cosine


def split_ring(values, theta):
    if len(values) == 1:
        return [(theta, values[0])]
    half = len(values) // 2
    cosine, sine = math.cos(theta / 2), math.sin(theta / 2)
    left, right = [], []
    for low, high in zip(values[:half], values[half:]):
        moved = complex_scale(high, cosine, sine)
        left.append((low[0] + moved[0], low[1] + moved[1]))
        right.append((low[0] - moved[0], low[1] - moved[1]))
    return split_ring(left, theta / 2) + split_ring(right, theta / 2 + math.pi)


def join_ring(values, theta):
    if len(values) == 1:
        return values
    half = len(values) // 2
    left = join_ring(values[:half], theta / 2)
    right = join_ring(values[half:], theta / 2 + math.pi)
    cosine, sine = math.cos(theta / 2), math.sin(theta / 2)
    low, high = [], []
    for one, two in zip(left, right):
        low.append((one[0] + two[0], one[1] + two[1]))
        high.append(complex_scale((one[0] - two[0], one[1] - two[1]), cosine, -sine))
    return low + high


def root_angles(count, theta):
    if count == 1:
        return [theta]
    return root_angles(count // 2, theta / 2) + root_angles(count // 2, theta / 2 + math.pi)


def mix(weights, values, dims):
    high, low = split_value(values)
    axis = dims[0][0]
    left = jnp.concatenate([weights[0], weights[0], weights[1]], axis=axis)
    return lax.dot_general(
        left, jnp.concatenate([high, low, high], axis=0), (dims, ((), ())), preferred_element_type=f32
    )


def tensor_kernel(spread, to_special, out):
    lane = lax.broadcasted_iota(jnp.int32, (8, LANES), 1)
    half = lane < 64
    sign = jnp.where(half, 1.0, -1.0).astype(f32)
    limb_low = (lane & 4) == 0
    comp = lax.broadcasted_iota(jnp.int32, (16, LANES), 1) & 3

    def roll(value, shift):
        return pltpu.roll(value, shift % LANES, 1)

    rows = jnp.concatenate([to_special[pl.ds(limb, 8, stride=2), :] for limb in range(2)], axis=0)
    old = lax.broadcasted_iota(jnp.int32, (16, 16), 0)
    new = lax.broadcasted_iota(jnp.int32, (16, 16), 1)
    order = jnp.where(old == 2 * (new & 7) + (new >> 3), 1.0, 0.0).astype(bf16)
    extend = split_value(
        sum(
            lax.dot_general(part, order, (((1,), (0,)), ((), ())), preferred_element_type=f32)
            for part in split_value(rows)
        )
    )
    table = spread[pl.ds(1, GROUPS, stride=2), :]
    shrink = split_value(jnp.concatenate([table[:, 16 * j : 16 * j + 16] for j in range(4)], axis=0))

    blocks = [spread[pl.ds(2 * GROUPS * c, GROUPS, stride=2), :] for c in range(COEF)]
    spectra = []
    for _, (real, imag) in split_ring(list(zip(blocks[: COEF // 2], blocks[COEF // 2 :])), math.pi / 2):
        one = real - roll(imag, 64)
        two = imag + roll(real, 64)
        spectra.append((jnp.where(half, one, two), jnp.where(half, two, one)))

    def tensor(value):
        left, right = [], []
        for part in value:
            after = roll(part, -1)
            left.append(jnp.where(comp == 1, after, jnp.where(comp == 3, roll(part, 3), part)))
            right.append(jnp.where((comp & 1) == 0, after, part))
        return (
            left[0] * right[0] - left[1] * right[1],
            left[0] * right[1] + left[1] * right[0],
        )

    owns = []
    for place in range(COEF // 4):
        for part in range(2):
            one, two = spectra[2 * place][part], spectra[2 * place + 1][part]
            owns.append(
                jnp.concatenate(
                    [jnp.where(limb_low, one, roll(two, 4)), jnp.where(limb_low, roll(one, -4), two)], axis=0
                )
            )
    specials = mix(extend, jnp.concatenate(owns, axis=1), ((1,), (0,)))
    own_products, special_products = [], []
    for place in range(COEF // 4):
        start = place * 2 * LANES
        own_products += tensor(owns[2 * place : 2 * place + 2])
        special_products += tensor(
            (specials[:, start : start + LANES], specials[:, start + LANES : start + 2 * LANES])
        )
    products = jnp.concatenate(
        [jnp.concatenate(own_products, axis=1), jnp.concatenate(special_products, axis=1)], axis=0
    )
    scaled = mix(shrink, products, ((0,), (0,)))
    mixed = []
    for place in range(COEF // 4):
        parts = []
        for part in range(2):
            start = (2 * place + part) * LANES
            low, high = scaled[:8, start : start + LANES], scaled[8:, start : start + LANES]
            parts.append((jnp.where(limb_low, low, roll(high, 4)), jnp.where(limb_low, roll(low, -4), high)))
        mixed.append((parts[0][0], parts[1][0]))
        mixed.append((parts[0][1], parts[1][1]))

    share = 1.0 / (COEF * BLOCK)
    joined = []
    for (real, imag), theta in zip(mixed, root_angles(COEF // 2, math.pi / 2)):
        cosine = share + sign * (share * math.sin(theta))
        sine = -share * math.cos(theta)
        own_real, own_imag = real * cosine - imag * sine, imag * cosine + real * sine
        other_real, other_imag = roll(own_real, 64), roll(own_imag, 64)
        joined.append(
            (
                jnp.where(half, own_real + other_real, own_imag + other_imag),
                jnp.where(half, own_imag - other_imag, own_real - other_real),
            )
        )
    for c, (real, imag) in enumerate(join_ring(joined, math.pi / 2)):
        out[GROUPS * c : GROUPS * (c + 1), :] = real
        out[GROUPS * (c + COEF // 2) : GROUPS * (c + COEF // 2 + 1), :] = imag


def restore_kernel(gathered, wide_high, wide_low, twiddle, out):
    row = lax.broadcasted_iota(jnp.int32, (8, LANES), 0)
    middle = (row & 3) == 1
    wide = (wide_high[...], wide_low[...])
    for pair in range(2):
        values = gathered[pair * LANES : (pair + 1) * LANES, :]
        spun = dot3(split_value(values), wide, ((0,), (0,)))
        real = spun[:64, :LANES] + spun[64:, LANES:]
        imag = spun[64:, :LANES] - spun[:64, LANES:]
        turned = []
        for k0 in range(K0):
            cosine = twiddle[k0 : k0 + 1, :]
            sine = twiddle[K0 + k0 : K0 + k0 + 1, :]
            own_real, own_imag = real[k0 * 8 : k0 * 8 + 8], imag[k0 * 8 : k0 * 8 + 8]
            turned.append((own_real * cosine + own_imag * sine, own_imag * cosine - own_real * sine))
        halves = []
        for k0 in range(K0 // 2):
            one, two = turned[k0], turned[k0 + K0 // 2]
            halves.append(((one[0] + two[0], one[1] + two[1]), (one[0] - two[0], one[1] - two[1])))
        for u in range(U):
            total = None
            for k0 in range(K0 // 2):
                cosine, sine = turn(u, k0)
                real_part, imag_part = halves[k0][u % 2]
                term = real_part if u == 0 else real_part * cosine + imag_part * sine
                total = term if total is None else total + term
            total = jnp.where(middle, total + pltpu.roll(total, 6, 0), total)
            for limb in range(2):
                for part in range(3):
                    row = limb * 4 + part
                    out[limb, part, pair : pair + 1, u * LANES : (u + 1) * LANES] = total[row : row + 1]


def in_vmem():
    return pl.BlockSpec(memory_space=pltpu.VMEM)


def in_hbm():
    return pl.BlockSpec(memory_space=pltpu.HBM)


def kept_far(*arrays):
    return [pltpu.with_memory_space_constraint(array, pltpu.HBM) for array in arrays]


def per_device(first_cipher, second_cipher, to_special, keep_table, scale_table):
    (wide_high, wide_low), twiddle = turn_tables()
    wide_high, wide_low, twiddle = jnp.asarray(wide_high), jnp.asarray(wide_low), jnp.asarray(twiddle)
    params = pltpu.CompilerParams(vmem_limit_bytes=32 * 1024 * 1024)
    spectra = pl.pallas_call(
        evaluate_kernel,
        out_shape=jax.ShapeDtypeStruct((2 * ROOTS, LANES), f32),
        in_specs=[in_hbm()] * 7,
        out_specs=in_vmem(),
        scratch_shapes=[
            pltpu.VMEM(first_cipher.shape, f32),
            pltpu.VMEM(second_cipher.shape, f32),
            pltpu.SMEM((2, 16), f32),
            pltpu.SMEM((2, 16), f32),
            pltpu.VMEM(wide_high.shape, bf16),
            pltpu.VMEM(wide_low.shape, bf16),
            pltpu.VMEM(twiddle.shape, f32),
            pltpu.VMEM((2 * U * 8, LANES), f32),
            pltpu.SemaphoreType.DMA((7,)),
        ],
        compiler_params=params,
        name="evaluate",
    )(*kept_far(first_cipher, second_cipher, keep_table.T, scale_table.T, wide_high, wide_low, twiddle))
    spread = lax.all_to_all(spectra.reshape(ROOTS, 2, LANES), ("coef", "limb"), 0, 0)
    scaled = pl.pallas_call(
        tensor_kernel,
        out_shape=jax.ShapeDtypeStruct((ROOTS, LANES), f32),
        in_specs=[in_vmem()] * 2,
        out_specs=in_vmem(),
        compiler_params=params,
        name="tensor",
    )(spread.reshape(2 * ROOTS, LANES), to_special)
    gathered = lax.all_to_all(scaled.reshape(ROOTS, 1, LANES), ("coef", "limb"), 0, 0)
    product = pl.pallas_call(
        restore_kernel,
        out_shape=jax.ShapeDtypeStruct((2, 3, 2, BLOCK), f32),
        in_specs=[in_vmem()] * 4,
        out_specs=in_vmem(),
        compiler_params=params,
        name="restore",
    )(gathered.reshape(ROOTS, LANES), wide_high, wide_low, twiddle)
    return product.transpose(0, 2, 1, 3)


def solution(mesh):
    return jax.shard_map(
        per_device,
        mesh=mesh,
        in_specs=(
            P("limb", None, None, "coef"),
            P("limb", None, None, "coef"),
            P(),
            P(None, "limb"),
            P(None, "limb"),
        ),
        out_specs=P("limb", None, None, "coef"),
        check_vma=False,
    )
```

```python
import math

import jax
import jax.numpy as jnp
import ml_dtypes
import numpy as np
from jax import lax
from jax.experimental import pallas as pl
from jax.experimental.pallas import tpu as pltpu
from jax.sharding import PartitionSpec as P

LANES = 128
U = 8
K0 = 8
BLOCK = U * LANES
COEF = 32
GROUPS = 8
ROOTS = 2 * LANES
f32 = jnp.float32
bf16 = jnp.bfloat16


def split_constant(values):
    high = values.astype(np.float32).astype(ml_dtypes.bfloat16)
    low = (values - high.astype(np.float64)).astype(ml_dtypes.bfloat16)
    return high, low


def turn_tables():
    index = np.arange(LANES)
    angle = 2 * np.pi * (index[:, None] * index[None, :] % LANES) / LANES
    wide = np.concatenate([np.cos(angle), np.sin(angle)], axis=1)
    v = np.arange(LANES)[None, :]
    k0 = np.arange(K0)[:, None]
    phase = np.pi * v * (4 * k0 + 1) / 2048
    twiddle = np.concatenate([np.cos(phase), np.sin(phase)], axis=0)
    return split_constant(wide), twiddle.astype(np.float32)


def split_value(values):
    high = values.astype(bf16)
    low = (values - high.astype(f32)).astype(bf16)
    return high, low


def dot3(left, right, dims):
    def one(a, b):
        return lax.dot_general(a, b, (dims, ((), ())), preferred_element_type=f32)

    return one(left[0], right[0]) + (one(left[0], right[1]) + one(left[1], right[0]))


def turn(u, k0):
    angle = math.pi * u * (4 * k0 + 1) / 16
    return math.cos(angle), math.sin(angle)


def evaluate_kernel(
    first_far, second_far, keep_far, scale_far, high_far, low_far, twiddle_far,
    out,
    first, second, keep, scale, wide_high, wide_low, twiddle, held, sems,
):
    copies = [
        pltpu.make_async_copy(far, near, sems.at[place])
        for place, (far, near) in enumerate(
            (
                (first_far, first),
                (second_far, second),
                (twiddle_far, twiddle),
                (high_far, wide_high),
                (low_far, wide_low),
                (keep_far, keep),
                (scale_far, scale),
            )
        )
    ]
    for copy in copies:
        copy.start()
    copies[0].wait()
    copies[1].wait()
    for pair in range(2):
        for u in range(U):
            base = (pair * U + u) * 8
            for limb in range(2):
                for cipher, ref in enumerate((first, second)):
                    held[pl.ds(base + limb * 4 + cipher, 2, stride=2), :] = ref[
                        limb, pair, :, u * LANES : (u + 1) * LANES
                    ]
    copies[2].wait()
    blocks = []
    for pair in range(2):
        parts = [held[(pair * U + u) * 8 : (pair * U + u + 1) * 8, :] for u in range(U)]
        spun = [None] * K0
        for k0 in range(K0 // 2):
            sums = []
            for start in (0, 1):
                real = imag = None
                for u in range(start, U, 2):
                    cosine, sine = turn(u, k0)
                    term_real = parts[u] if u == 0 else parts[u] * cosine
                    real = term_real if real is None else real + term_real
                    if u:
                        term_imag = parts[u] * sine
                        imag = term_imag if imag is None else imag + term_imag
                sums.append((real, imag))
            (even_real, even_imag), (odd_real, odd_imag) = sums
            spun[k0] = (even_real + odd_real, even_imag + odd_imag)
            spun[k0 + K0 // 2] = (even_real - odd_real, even_imag - odd_imag)
        reals, imags = [], []
        for k0 in range(K0):
            cosine = twiddle[k0 : k0 + 1, :]
            sine = twiddle[K0 + k0 : K0 + k0 + 1, :]
            real, imag = spun[k0]
            reals.append(real * cosine - imag * sine)
            imags.append(real * sine + imag * cosine)
        real = jnp.concatenate(reals, axis=0)
        imag = jnp.concatenate(imags, axis=0)
        blocks.append(jnp.concatenate([real, -imag], axis=1))
        blocks.append(jnp.concatenate([imag, real], axis=1))
    rows = jnp.concatenate(blocks, axis=0)
    copies[3].wait()
    copies[4].wait()
    parted = split_value(rows)
    spectrum = lax.dot_general(
        jnp.concatenate([wide_high[...], wide_high[...], wide_low[...]], axis=1),
        jnp.concatenate([parted[0], parted[1], parted[0]], axis=1),
        (((1,), (1,)), ((), ())),
        preferred_element_type=f32,
    )
    copies[5].wait()
    copies[6].wait()
    lane = lax.broadcasted_iota(jnp.int32, (8, LANES), 1)
    table = jnp.zeros((8, LANES), f32)
    for i in range(16):
        for limb in range(2):
            place = limb * 16 + (i % 2) * 8 + i // 2
            table = jnp.where(lane == place, keep[limb, i], table)
            table = jnp.where(lane == 32 + place, scale[limb, i], table)
    for pair in range(2):
        out[pl.ds(pair * 256, LANES, stride=2), :] = spectrum[:, pair * LANES : (pair + 1) * LANES]
    for tile in range(ROOTS // 8):
        out[pl.ds(tile * 16 + 1, 8, stride=2), :] = table


def complex_scale(value, cosine, sine):
    real, imag = value
    if abs(cosine) < 1e-9:
        return (-imag, real) if sine > 0 else (imag, -real)
    if abs(abs(cosine) - abs(sine)) < 1e-9:
        if cosine * sine > 0:
            return (real - imag) * cosine, (real + imag) * cosine
        return (real + imag) * cosine, (imag - real) * cosine
    return real * cosine - imag * sine, real * sine + imag * cosine


def split_ring(values, theta):
    if len(values) == 1:
        return [(theta, values[0])]
    half = len(values) // 2
    cosine, sine = math.cos(theta / 2), math.sin(theta / 2)
    left, right = [], []
    for low, high in zip(values[:half], values[half:]):
        moved = complex_scale(high, cosine, sine)
        left.append((low[0] + moved[0], low[1] + moved[1]))
        right.append((low[0] - moved[0], low[1] - moved[1]))
    return split_ring(left, theta / 2) + split_ring(right, theta / 2 + math.pi)


def join_ring(values, theta):
    if len(values) == 1:
        return values
    half = len(values) // 2
    left = join_ring(values[:half], theta / 2)
    right = join_ring(values[half:], theta / 2 + math.pi)
    cosine, sine = math.cos(theta / 2), math.sin(theta / 2)
    low, high = [], []
    for one, two in zip(left, right):
        low.append((one[0] + two[0], one[1] + two[1]))
        high.append(complex_scale((one[0] - two[0], one[1] - two[1]), cosine, -sine))
    return low + high


def root_angles(count, theta):
    if count == 1:
        return [theta]
    return root_angles(count // 2, theta / 2) + root_angles(count // 2, theta / 2 + math.pi)


def mix(weights, values, dims):
    high, low = split_value(values)
    axis = dims[0][0]
    left = jnp.concatenate([weights[0], weights[0], weights[1]], axis=axis)
    return lax.dot_general(
        left, jnp.concatenate([high, low, high], axis=0), (dims, ((), ())), preferred_element_type=f32
    )


def tensor_kernel(spread, to_special, out):
    lane = lax.broadcasted_iota(jnp.int32, (8, LANES), 1)
    half = lane < 64
    sign = jnp.where(half, 1.0, -1.0).astype(f32)
    limb_low = (lane & 4) == 0
    comp = lax.broadcasted_iota(jnp.int32, (16, LANES), 1) & 3

    def roll(value, shift):
        return pltpu.roll(value, shift % LANES, 1)

    rows = jnp.concatenate([to_special[pl.ds(limb, 8, stride=2), :] for limb in range(2)], axis=0)
    old = lax.broadcasted_iota(jnp.int32, (16, 16), 0)
    new = lax.broadcasted_iota(jnp.int32, (16, 16), 1)
    order = jnp.where(old == 2 * (new & 7) + (new >> 3), 1.0, 0.0).astype(bf16)
    extend = split_value(
        sum(
            lax.dot_general(part, order, (((1,), (0,)), ((), ())), preferred_element_type=f32)
            for part in split_value(rows)
        )
    )
    table = spread[pl.ds(1, GROUPS, stride=2 * COEF), :]
    shrink = split_value(jnp.concatenate([table[:, 16 * j : 16 * j + 16] for j in range(4)], axis=0))

    blocks = [spread[pl.ds(2 * c, GROUPS, stride=2 * COEF), :] for c in range(COEF)]
    spectra = []
    for _, (real, imag) in split_ring(list(zip(blocks[: COEF // 2], blocks[COEF // 2 :])), math.pi / 2):
        one = real - roll(imag, 64)
        two = imag + roll(real, 64)
        spectra.append((jnp.where(half, one, two), jnp.where(half, two, one)))

    def tensor(value):
        left, right = [], []
        for part in value:
            after = roll(part, -1)
            left.append(jnp.where(comp == 1, after, jnp.where(comp == 3, roll(part, 3), part)))
            right.append(jnp.where((comp & 1) == 0, after, part))
        return (
            left[0] * right[0] - left[1] * right[1],
            left[0] * right[1] + left[1] * right[0],
        )

    owns = []
    for place in range(COEF // 4):
        for part in range(2):
            one, two = spectra[2 * place][part], spectra[2 * place + 1][part]
            owns.append(
                jnp.concatenate(
                    [jnp.where(limb_low, one, roll(two, 4)), jnp.where(limb_low, roll(one, -4), two)], axis=0
                )
            )
    specials = mix(extend, jnp.concatenate(owns, axis=1), ((1,), (0,)))
    own_products, special_products = [], []
    for place in range(COEF // 4):
        start = place * 2 * LANES
        own_products += tensor(owns[2 * place : 2 * place + 2])
        special_products += tensor(
            (specials[:, start : start + LANES], specials[:, start + LANES : start + 2 * LANES])
        )
    products = jnp.concatenate(
        [jnp.concatenate(own_products, axis=1), jnp.concatenate(special_products, axis=1)], axis=0
    )
    scaled = mix(shrink, products, ((0,), (0,)))
    mixed = []
    for place in range(COEF // 4):
        parts = []
        for part in range(2):
            start = (2 * place + part) * LANES
            low, high = scaled[:8, start : start + LANES], scaled[8:, start : start + LANES]
            parts.append((jnp.where(limb_low, low, roll(high, 4)), jnp.where(limb_low, roll(low, -4), high)))
        mixed.append((parts[0][0], parts[1][0]))
        mixed.append((parts[0][1], parts[1][1]))

    share = 1.0 / (COEF * BLOCK)
    joined = []
    for (real, imag), theta in zip(mixed, root_angles(COEF // 2, math.pi / 2)):
        cosine = share + sign * (share * math.sin(theta))
        sine = -share * math.cos(theta)
        own_real, own_imag = real * cosine - imag * sine, imag * cosine + real * sine
        other_real, other_imag = roll(own_real, 64), roll(own_imag, 64)
        joined.append(
            (
                jnp.where(half, own_real + other_real, own_imag + other_imag),
                jnp.where(half, own_imag - other_imag, own_real - other_real),
            )
        )
    for c, (real, imag) in enumerate(join_ring(joined, math.pi / 2)):
        out[pl.ds(c, GROUPS, stride=COEF), :] = real
        out[pl.ds(c + COEF // 2, GROUPS, stride=COEF), :] = imag


def restore_kernel(gathered, wide_high, wide_low, twiddle, out):
    row = lax.broadcasted_iota(jnp.int32, (8, LANES), 0)
    middle = (row & 3) == 1
    values = split_value(jnp.concatenate([gathered[:LANES, :], gathered[LANES:, :]], axis=1))
    left = jnp.concatenate([values[0], values[1], values[0]], axis=0)
    right = jnp.concatenate([wide_high[...], wide_high[...], wide_low[...]], axis=0)
    both = lax.dot_general(left, right, (((0,), (0,)), ((), ())), preferred_element_type=f32)
    for pair in range(2):
        spun = both[pair * LANES : (pair + 1) * LANES]
        real = spun[:64, :LANES] + spun[64:, LANES:]
        imag = spun[64:, :LANES] - spun[:64, LANES:]
        turned = []
        for k0 in range(K0):
            cosine = twiddle[k0 : k0 + 1, :]
            sine = twiddle[K0 + k0 : K0 + k0 + 1, :]
            own_real, own_imag = real[k0 * 8 : k0 * 8 + 8], imag[k0 * 8 : k0 * 8 + 8]
            turned.append((own_real * cosine + own_imag * sine, own_imag * cosine - own_real * sine))
        halves = []
        for k0 in range(K0 // 2):
            one, two = turned[k0], turned[k0 + K0 // 2]
            halves.append(((one[0] + two[0], one[1] + two[1]), (one[0] - two[0], one[1] - two[1])))
        for u in range(U):
            total = None
            for k0 in range(K0 // 2):
                cosine, sine = turn(u, k0)
                real_part, imag_part = halves[k0][u % 2]
                term = real_part if u == 0 else real_part * cosine + imag_part * sine
                total = term if total is None else total + term
            total = jnp.where(middle, total + pltpu.roll(total, 6, 0), total)
            for limb in range(2):
                for part in range(3):
                    row = limb * 4 + part
                    out[limb, part, pair : pair + 1, u * LANES : (u + 1) * LANES] = total[row : row + 1]


def in_vmem():
    return pl.BlockSpec(memory_space=pltpu.VMEM)


def in_hbm():
    return pl.BlockSpec(memory_space=pltpu.HBM)


def kept_far(*arrays):
    return [pltpu.with_memory_space_constraint(array, pltpu.HBM) for array in arrays]


def per_device(first_cipher, second_cipher, to_special, keep_table, scale_table):
    (wide_high, wide_low), twiddle = turn_tables()
    wide_high, wide_low, twiddle = jnp.asarray(wide_high), jnp.asarray(wide_low), jnp.asarray(twiddle)
    params = pltpu.CompilerParams(vmem_limit_bytes=32 * 1024 * 1024)
    spectra = pl.pallas_call(
        evaluate_kernel,
        out_shape=jax.ShapeDtypeStruct((2 * ROOTS, LANES), f32),
        in_specs=[in_hbm()] * 7,
        out_specs=in_vmem(),
        scratch_shapes=[
            pltpu.VMEM(first_cipher.shape, f32),
            pltpu.VMEM(second_cipher.shape, f32),
            pltpu.SMEM((2, 16), f32),
            pltpu.SMEM((2, 16), f32),
            pltpu.VMEM(wide_high.shape, bf16),
            pltpu.VMEM(wide_low.shape, bf16),
            pltpu.VMEM(twiddle.shape, f32),
            pltpu.VMEM((2 * U * 8, LANES), f32),
            pltpu.SemaphoreType.DMA((7,)),
        ],
        compiler_params=params,
        name="evaluate",
    )(*kept_far(first_cipher, second_cipher, keep_table.T, scale_table.T, wide_high, wide_low, twiddle))
    spread = lax.all_to_all(spectra.reshape(ROOTS, 2, LANES), ("limb", "coef"), 0, 0)
    scaled = pl.pallas_call(
        tensor_kernel,
        out_shape=jax.ShapeDtypeStruct((ROOTS, LANES), f32),
        in_specs=[in_vmem()] * 2,
        out_specs=in_vmem(),
        compiler_params=params,
        name="tensor",
    )(spread.reshape(2 * ROOTS, LANES), to_special)
    gathered = lax.all_to_all(scaled.reshape(ROOTS, 1, LANES), ("limb", "coef"), 0, 0)
    product = pl.pallas_call(
        restore_kernel,
        out_shape=jax.ShapeDtypeStruct((2, 3, 2, BLOCK), f32),
        in_specs=[in_vmem()] * 4,
        out_specs=in_vmem(),
        compiler_params=params,
        name="restore",
    )(gathered.reshape(ROOTS, LANES), wide_high, wide_low, twiddle)
    return product.transpose(0, 2, 1, 3)


def solution(mesh):
    return jax.shard_map(
        per_device,
        mesh=mesh,
        in_specs=(
            P("limb", None, None, "coef"),
            P("limb", None, None, "coef"),
            P(),
            P(None, "limb"),
            P(None, "limb"),
        ),
        out_specs=P("limb", None, None, "coef"),
        check_vma=False,
    )
```

```python
import math

import jax
import jax.numpy as jnp
import ml_dtypes
import numpy as np
from jax import lax
from jax.experimental import pallas as pl
from jax.experimental.pallas import tpu as pltpu
from jax.sharding import PartitionSpec as P

LANES = 128
U = 8
K0 = 8
BLOCK = U * LANES
COEF = 32
GROUPS = 8
ROOTS = 2 * LANES
f32 = jnp.float32
bf16 = jnp.bfloat16


def split_constant(values):
    high = values.astype(np.float32).astype(ml_dtypes.bfloat16)
    low = (values - high.astype(np.float64)).astype(ml_dtypes.bfloat16)
    return high, low


def turn_tables():
    index = np.arange(LANES)
    angle = 2 * np.pi * (index[:, None] * index[None, :] % LANES) / LANES
    wide = np.concatenate([np.cos(angle), np.sin(angle)], axis=1)
    v = np.arange(LANES)[None, :]
    k0 = np.arange(K0)[:, None]
    phase = np.pi * v * (4 * k0 + 1) / 2048
    twiddle = np.concatenate([np.cos(phase), np.sin(phase)], axis=0)
    return split_constant(wide), twiddle.astype(np.float32)


def split_value(values):
    high = values.astype(bf16)
    low = (values - high.astype(f32)).astype(bf16)
    return high, low


def dot3(left, right, dims):
    def one(a, b):
        return lax.dot_general(a, b, (dims, ((), ())), preferred_element_type=f32)

    return one(left[0], right[0]) + (one(left[0], right[1]) + one(left[1], right[0]))


def turn(u, k0):
    angle = math.pi * u * (4 * k0 + 1) / 16
    return math.cos(angle), math.sin(angle)


def evaluate_kernel(
    first_far, second_far, keep_far, scale_far, high_far, low_far, twiddle_far,
    out,
    first, second, keep, scale, wide_high, wide_low, twiddle, held, sems,
):
    copies = [
        pltpu.make_async_copy(far, near, sems.at[place])
        for place, (far, near) in enumerate(
            (
                (first_far, first),
                (second_far, second),
                (twiddle_far, twiddle),
                (high_far, wide_high),
                (low_far, wide_low),
                (keep_far, keep),
                (scale_far, scale),
            )
        )
    ]
    for copy in copies:
        copy.start()
    copies[0].wait()
    copies[1].wait()
    for pair in range(2):
        for u in range(U):
            base = (pair * U + u) * 8
            for limb in range(2):
                for cipher, ref in enumerate((first, second)):
                    held[pl.ds(base + limb * 4 + cipher, 2, stride=2), :] = ref[
                        limb, pair, :, u * LANES : (u + 1) * LANES
                    ]
    copies[2].wait()
    copies[5].wait()
    copies[6].wait()
    lane = lax.broadcasted_iota(jnp.int32, (8, LANES), 1)
    table = jnp.zeros((8, LANES), f32)
    for i in range(16):
        for limb in range(2):
            place = limb * 16 + (i % 2) * 8 + i // 2
            table = jnp.where(lane == place, keep[limb, i], table)
            table = jnp.where(lane == 32 + place, scale[limb, i], table)
    for tile in range(ROOTS // 8):
        out[pl.ds(tile * 16 + 1, 8, stride=2), :] = table
    blocks = []
    for pair in range(2):
        parts = [held[(pair * U + u) * 8 : (pair * U + u + 1) * 8, :] for u in range(U)]
        spun = [None] * K0
        for k0 in range(K0 // 2):
            sums = []
            for start in (0, 1):
                real = imag = None
                for u in range(start, U, 2):
                    cosine, sine = turn(u, k0)
                    term_real = parts[u] if u == 0 else parts[u] * cosine
                    real = term_real if real is None else real + term_real
                    if u:
                        term_imag = parts[u] * sine
                        imag = term_imag if imag is None else imag + term_imag
                sums.append((real, imag))
            (even_real, even_imag), (odd_real, odd_imag) = sums
            spun[k0] = (even_real + odd_real, even_imag + odd_imag)
            spun[k0 + K0 // 2] = (even_real - odd_real, even_imag - odd_imag)
        reals, imags = [], []
        for k0 in range(K0):
            cosine = twiddle[k0 : k0 + 1, :]
            sine = twiddle[K0 + k0 : K0 + k0 + 1, :]
            real, imag = spun[k0]
            reals.append(real * cosine - imag * sine)
            imags.append(real * sine + imag * cosine)
        real = jnp.concatenate(reals, axis=0)
        imag = jnp.concatenate(imags, axis=0)
        blocks.append(jnp.concatenate([real, -imag], axis=1))
        blocks.append(jnp.concatenate([imag, real], axis=1))
    rows = jnp.concatenate(blocks, axis=0)
    copies[3].wait()
    copies[4].wait()
    parted = split_value(rows)
    spectrum = lax.dot_general(
        jnp.concatenate([wide_high[...], wide_high[...], wide_low[...]], axis=1),
        jnp.concatenate([parted[0], parted[1], parted[0]], axis=1),
        (((1,), (1,)), ((), ())),
        preferred_element_type=f32,
    )
    for pair in range(2):
        out[pl.ds(pair * 256, LANES, stride=2), :] = spectrum[:, pair * LANES : (pair + 1) * LANES]


def complex_scale(value, cosine, sine):
    real, imag = value
    if abs(cosine) < 1e-9:
        return (-imag, real) if sine > 0 else (imag, -real)
    if abs(abs(cosine) - abs(sine)) < 1e-9:
        if cosine * sine > 0:
            return (real - imag) * cosine, (real + imag) * cosine
        return (real + imag) * cosine, (imag - real) * cosine
    return real * cosine - imag * sine, real * sine + imag * cosine


def split_ring(values, theta):
    if len(values) == 1:
        return [(theta, values[0])]
    half = len(values) // 2
    cosine, sine = math.cos(theta / 2), math.sin(theta / 2)
    left, right = [], []
    for low, high in zip(values[:half], values[half:]):
        moved = complex_scale(high, cosine, sine)
        left.append((low[0] + moved[0], low[1] + moved[1]))
        right.append((low[0] - moved[0], low[1] - moved[1]))
    return split_ring(left, theta / 2) + split_ring(right, theta / 2 + math.pi)


def join_ring(values, theta):
    if len(values) == 1:
        return values
    half = len(values) // 2
    left = join_ring(values[:half], theta / 2)
    right = join_ring(values[half:], theta / 2 + math.pi)
    cosine, sine = math.cos(theta / 2), math.sin(theta / 2)
    low, high = [], []
    for one, two in zip(left, right):
        low.append((one[0] + two[0], one[1] + two[1]))
        high.append(complex_scale((one[0] - two[0], one[1] - two[1]), cosine, -sine))
    return low + high


def root_angles(count, theta):
    if count == 1:
        return [theta]
    return root_angles(count // 2, theta / 2) + root_angles(count // 2, theta / 2 + math.pi)


def mix(weights, values, dims):
    high, low = split_value(values)
    axis = dims[0][0]
    left = jnp.concatenate([weights[0], weights[0], weights[1]], axis=axis)
    return lax.dot_general(
        left, jnp.concatenate([high, low, high], axis=0), (dims, ((), ())), preferred_element_type=f32
    )


def tensor_kernel(spread, to_special, out):
    lane = lax.broadcasted_iota(jnp.int32, (8, LANES), 1)
    half = lane < 64
    sign = jnp.where(half, 1.0, -1.0).astype(f32)
    limb_low = (lane & 4) == 0
    comp = lax.broadcasted_iota(jnp.int32, (16, LANES), 1) & 3

    def roll(value, shift):
        return pltpu.roll(value, shift % LANES, 1)

    rows = jnp.concatenate([to_special[pl.ds(limb, 8, stride=2), :] for limb in range(2)], axis=0)
    old = lax.broadcasted_iota(jnp.int32, (16, 16), 0)
    new = lax.broadcasted_iota(jnp.int32, (16, 16), 1)
    order = jnp.where(old == 2 * (new & 7) + (new >> 3), 1.0, 0.0).astype(bf16)
    extend = split_value(
        sum(
            lax.dot_general(part, order, (((1,), (0,)), ((), ())), preferred_element_type=f32)
            for part in split_value(rows)
        )
    )
    table = spread[pl.ds(1, GROUPS, stride=2 * COEF), :]
    shrink = split_value(jnp.concatenate([table[:, 16 * j : 16 * j + 16] for j in range(4)], axis=0))

    blocks = [spread[pl.ds(2 * c, GROUPS, stride=2 * COEF), :] for c in range(COEF)]
    spectra = []
    for _, (real, imag) in split_ring(list(zip(blocks[: COEF // 2], blocks[COEF // 2 :])), math.pi / 2):
        one = real - roll(imag, 64)
        two = imag + roll(real, 64)
        spectra.append((jnp.where(half, one, two), jnp.where(half, two, one)))

    def tensor(value):
        left, right = [], []
        for part in value:
            after = roll(part, -1)
            left.append(jnp.where(comp == 1, after, jnp.where(comp == 3, roll(part, 3), part)))
            right.append(jnp.where((comp & 1) == 0, after, part))
        return (
            left[0] * right[0] - left[1] * right[1],
            left[0] * right[1] + left[1] * right[0],
        )

    owns = []
    for place in range(COEF // 4):
        for part in range(2):
            one, two = spectra[2 * place][part], spectra[2 * place + 1][part]
            owns.append(
                jnp.concatenate(
                    [jnp.where(limb_low, one, roll(two, 4)), jnp.where(limb_low, roll(one, -4), two)], axis=0
                )
            )
    specials = mix(extend, jnp.concatenate(owns, axis=1), ((1,), (0,)))
    own_products, special_products = [], []
    for place in range(COEF // 4):
        start = place * 2 * LANES
        own_products += tensor(owns[2 * place : 2 * place + 2])
        special_products += tensor(
            (specials[:, start : start + LANES], specials[:, start + LANES : start + 2 * LANES])
        )
    products = jnp.concatenate(
        [jnp.concatenate(own_products, axis=1), jnp.concatenate(special_products, axis=1)], axis=0
    )
    scaled = mix(shrink, products, ((0,), (0,)))
    mixed = []
    for place in range(COEF // 4):
        parts = []
        for part in range(2):
            start = (2 * place + part) * LANES
            low, high = scaled[:8, start : start + LANES], scaled[8:, start : start + LANES]
            parts.append((jnp.where(limb_low, low, roll(high, 4)), jnp.where(limb_low, roll(low, -4), high)))
        mixed.append((parts[0][0], parts[1][0]))
        mixed.append((parts[0][1], parts[1][1]))

    share = 1.0 / (COEF * BLOCK)
    joined = []
    for (real, imag), theta in zip(mixed, root_angles(COEF // 2, math.pi / 2)):
        cosine = share + sign * (share * math.sin(theta))
        sine = -share * math.cos(theta)
        own_real, own_imag = real * cosine - imag * sine, imag * cosine + real * sine
        other_real, other_imag = roll(own_real, 64), roll(own_imag, 64)
        joined.append(
            (
                jnp.where(half, own_real + other_real, own_imag + other_imag),
                jnp.where(half, own_imag - other_imag, own_real - other_real),
            )
        )
    for c, (real, imag) in enumerate(join_ring(joined, math.pi / 2)):
        out[pl.ds(c, GROUPS, stride=COEF), :] = real
        out[pl.ds(c + COEF // 2, GROUPS, stride=COEF), :] = imag


def restore_kernel(gathered, wide_high, wide_low, twiddle, out):
    row = lax.broadcasted_iota(jnp.int32, (8, LANES), 0)
    middle = (row & 3) == 1
    values = split_value(jnp.concatenate([gathered[:LANES, :], gathered[LANES:, :]], axis=1))
    left = jnp.concatenate([values[0], values[1], values[0]], axis=0)
    right = jnp.concatenate([wide_high[...], wide_high[...], wide_low[...]], axis=0)
    both = lax.dot_general(left, right, (((0,), (0,)), ((), ())), preferred_element_type=f32)
    for pair in range(2):
        spun = both[pair * LANES : (pair + 1) * LANES]
        real = spun[:64, :LANES] + spun[64:, LANES:]
        imag = spun[64:, :LANES] - spun[:64, LANES:]
        turned = []
        for k0 in range(K0):
            cosine = twiddle[k0 : k0 + 1, :]
            sine = twiddle[K0 + k0 : K0 + k0 + 1, :]
            own_real, own_imag = real[k0 * 8 : k0 * 8 + 8], imag[k0 * 8 : k0 * 8 + 8]
            turned.append((own_real * cosine + own_imag * sine, own_imag * cosine - own_real * sine))
        halves = []
        for k0 in range(K0 // 2):
            one, two = turned[k0], turned[k0 + K0 // 2]
            halves.append(((one[0] + two[0], one[1] + two[1]), (one[0] - two[0], one[1] - two[1])))
        for u in range(U):
            total = None
            for k0 in range(K0 // 2):
                cosine, sine = turn(u, k0)
                real_part, imag_part = halves[k0][u % 2]
                term = real_part if u == 0 else real_part * cosine + imag_part * sine
                total = term if total is None else total + term
            total = jnp.where(middle, total + pltpu.roll(total, 6, 0), total)
            for limb in range(2):
                for part in range(3):
                    row = limb * 4 + part
                    out[limb, part, pair : pair + 1, u * LANES : (u + 1) * LANES] = total[row : row + 1]


def in_vmem():
    return pl.BlockSpec(memory_space=pltpu.VMEM)


def in_hbm():
    return pl.BlockSpec(memory_space=pltpu.HBM)


def kept_far(*arrays):
    return [pltpu.with_memory_space_constraint(array, pltpu.HBM) for array in arrays]


def per_device(first_cipher, second_cipher, to_special, keep_table, scale_table):
    (wide_high, wide_low), twiddle = turn_tables()
    wide_high, wide_low, twiddle = jnp.asarray(wide_high), jnp.asarray(wide_low), jnp.asarray(twiddle)
    params = pltpu.CompilerParams(vmem_limit_bytes=32 * 1024 * 1024)
    spectra = pl.pallas_call(
        evaluate_kernel,
        out_shape=jax.ShapeDtypeStruct((2 * ROOTS, LANES), f32),
        in_specs=[in_hbm()] * 7,
        out_specs=in_vmem(),
        scratch_shapes=[
            pltpu.VMEM(first_cipher.shape, f32),
            pltpu.VMEM(second_cipher.shape, f32),
            pltpu.SMEM((2, 16), f32),
            pltpu.SMEM((2, 16), f32),
            pltpu.VMEM(wide_high.shape, bf16),
            pltpu.VMEM(wide_low.shape, bf16),
            pltpu.VMEM(twiddle.shape, f32),
            pltpu.VMEM((2 * U * 8 + 16, LANES), f32),
            pltpu.SemaphoreType.DMA((7,)),
        ],
        compiler_params=params,
        name="evaluate",
    )(*kept_far(first_cipher, second_cipher, keep_table.T, scale_table.T, wide_high, wide_low, twiddle))
    spread = lax.all_to_all(spectra.reshape(ROOTS, 2, LANES), ("limb", "coef"), 0, 0)
    scaled = pl.pallas_call(
        tensor_kernel,
        out_shape=jax.ShapeDtypeStruct((ROOTS, LANES), f32),
        in_specs=[in_vmem()] * 2,
        out_specs=in_vmem(),
        compiler_params=params,
        name="tensor",
    )(spread.reshape(2 * ROOTS, LANES), to_special)
    gathered = lax.all_to_all(scaled.reshape(ROOTS, 1, LANES), ("limb", "coef"), 0, 0)
    product = pl.pallas_call(
        restore_kernel,
        out_shape=jax.ShapeDtypeStruct((2, 3, 2, BLOCK), f32),
        in_specs=[in_vmem()] * 4,
        out_specs=in_vmem(),
        compiler_params=params,
        name="restore",
    )(gathered.reshape(ROOTS, LANES), wide_high, wide_low, twiddle)
    return product.transpose(0, 2, 1, 3)


def solution(mesh):
    return jax.shard_map(
        per_device,
        mesh=mesh,
        in_specs=(
            P("limb", None, None, "coef"),
            P("limb", None, None, "coef"),
            P(),
            P(None, "limb"),
            P(None, "limb"),
        ),
        out_specs=P("limb", None, None, "coef"),
        check_vma=False,
    )
```

```python
import math

import jax
import jax.numpy as jnp
import ml_dtypes
import numpy as np
from jax import lax
from jax.experimental import pallas as pl
from jax.experimental.pallas import tpu as pltpu
from jax.sharding import PartitionSpec as P

LANES = 128
U = 8
K0 = 8
BLOCK = U * LANES
COEF = 32
GROUPS = 8
ROOTS = 2 * LANES
f32 = jnp.float32
bf16 = jnp.bfloat16


def split_constant(values):
    high = values.astype(np.float32).astype(ml_dtypes.bfloat16)
    low = (values - high.astype(np.float64)).astype(ml_dtypes.bfloat16)
    return high, low


def turn_tables():
    index = np.arange(LANES)
    angle = 2 * np.pi * (index[:, None] * index[None, :] % LANES) / LANES
    wide = np.concatenate([np.cos(angle), np.sin(angle)], axis=1)
    v = np.arange(LANES)[None, :]
    k0 = np.arange(K0)[:, None]
    phase = np.pi * v * (4 * k0 + 1) / 2048
    twiddle = np.concatenate([np.cos(phase), np.sin(phase)], axis=0)
    return split_constant(wide), twiddle.astype(np.float32)


def split_value(values):
    high = values.astype(bf16)
    low = (values - high.astype(f32)).astype(bf16)
    return high, low


def dot3(left, right, dims):
    def one(a, b):
        return lax.dot_general(a, b, (dims, ((), ())), preferred_element_type=f32)

    return one(left[0], right[0]) + (one(left[0], right[1]) + one(left[1], right[0]))


def turn(u, k0):
    angle = math.pi * u * (4 * k0 + 1) / 16
    return math.cos(angle), math.sin(angle)


def evaluate_kernel(
    first_far, second_far, keep_far, scale_far, high_far, low_far, twiddle_far,
    out,
    first, second, keep, scale, wide_high, wide_low, twiddle, held, sems,
):
    copies = [
        pltpu.make_async_copy(far, near, sems.at[place])
        for place, (far, near) in enumerate(
            (
                (first_far, first),
                (second_far, second),
                (twiddle_far, twiddle),
                (high_far, wide_high),
                (low_far, wide_low),
                (keep_far, keep),
                (scale_far, scale),
            )
        )
    ]
    for copy in copies:
        copy.start()
    copies[0].wait()
    copies[1].wait()
    for pair in range(2):
        for u in range(U):
            base = (pair * U + u) * 8
            for limb in range(2):
                for cipher, ref in enumerate((first, second)):
                    held[pl.ds(base + limb * 4 + cipher, 2, stride=2), :] = ref[
                        limb, pair, :, u * LANES : (u + 1) * LANES
                    ]
    copies[2].wait()
    copies[5].wait()
    copies[6].wait()
    lane = lax.broadcasted_iota(jnp.int32, (8, LANES), 1)
    table = jnp.zeros((8, LANES), f32)
    for i in range(16):
        for limb in range(2):
            place = limb * 16 + (i % 2) * 8 + i // 2
            table = jnp.where(lane == place, keep[limb, i], table)
            table = jnp.where(lane == 32 + place, scale[limb, i], table)
    for tile in range(ROOTS // 8):
        out[pl.ds(tile * 16 + 1, 8, stride=2), :] = table
    blocks = []
    for pair in range(2):
        parts = [held[(pair * U + u) * 8 : (pair * U + u + 1) * 8, :] for u in range(U)]
        spun = [None] * K0
        for k0 in range(K0 // 2):
            sums = []
            for start in (0, 1):
                real = imag = None
                for u in range(start, U, 2):
                    cosine, sine = turn(u, k0)
                    term_real = parts[u] if u == 0 else parts[u] * cosine
                    real = term_real if real is None else real + term_real
                    if u:
                        term_imag = parts[u] * sine
                        imag = term_imag if imag is None else imag + term_imag
                sums.append((real, imag))
            (even_real, even_imag), (odd_real, odd_imag) = sums
            spun[k0] = (even_real + odd_real, even_imag + odd_imag)
            spun[k0 + K0 // 2] = (even_real - odd_real, even_imag - odd_imag)
        reals, imags = [], []
        for k0 in range(K0):
            cosine = twiddle[k0 : k0 + 1, :]
            sine = twiddle[K0 + k0 : K0 + k0 + 1, :]
            real, imag = spun[k0]
            reals.append(real * cosine - imag * sine)
            imags.append(real * sine + imag * cosine)
        real = jnp.concatenate(reals, axis=0)
        imag = jnp.concatenate(imags, axis=0)
        blocks.append(jnp.concatenate([real, -imag], axis=1))
        blocks.append(jnp.concatenate([imag, real], axis=1))
    rows = jnp.concatenate(blocks, axis=0)
    copies[3].wait()
    copies[4].wait()
    left = jnp.concatenate([wide_high[...], wide_high[...], wide_low[...]], axis=1)
    halves = []
    for pair in range(2):
        high, low = split_value(jnp.concatenate(blocks[2 * pair : 2 * pair + 2], axis=0))
        halves.append(
            lax.dot_general(
                left, jnp.concatenate([high, low, high], axis=1), (((1,), (1,)), ((), ())), preferred_element_type=f32
            )
        )
    spectrum = jnp.concatenate(halves, axis=1)
    for pair in range(2):
        out[pl.ds(pair * 256, LANES, stride=2), :] = spectrum[:, pair * LANES : (pair + 1) * LANES]


def complex_scale(value, cosine, sine):
    real, imag = value
    if abs(cosine) < 1e-9:
        return (-imag, real) if sine > 0 else (imag, -real)
    if abs(abs(cosine) - abs(sine)) < 1e-9:
        if cosine * sine > 0:
            return (real - imag) * cosine, (real + imag) * cosine
        return (real + imag) * cosine, (imag - real) * cosine
    return real * cosine - imag * sine, real * sine + imag * cosine


def split_ring(values, theta):
    if len(values) == 1:
        return [(theta, values[0])]
    half = len(values) // 2
    cosine, sine = math.cos(theta / 2), math.sin(theta / 2)
    left, right = [], []
    for low, high in zip(values[:half], values[half:]):
        moved = complex_scale(high, cosine, sine)
        left.append((low[0] + moved[0], low[1] + moved[1]))
        right.append((low[0] - moved[0], low[1] - moved[1]))
    return split_ring(left, theta / 2) + split_ring(right, theta / 2 + math.pi)


def join_ring(values, theta):
    if len(values) == 1:
        return values
    half = len(values) // 2
    left = join_ring(values[:half], theta / 2)
    right = join_ring(values[half:], theta / 2 + math.pi)
    cosine, sine = math.cos(theta / 2), math.sin(theta / 2)
    low, high = [], []
    for one, two in zip(left, right):
        low.append((one[0] + two[0], one[1] + two[1]))
        high.append(complex_scale((one[0] - two[0], one[1] - two[1]), cosine, -sine))
    return low + high


def root_angles(count, theta):
    if count == 1:
        return [theta]
    return root_angles(count // 2, theta / 2) + root_angles(count // 2, theta / 2 + math.pi)


def mix(weights, values, dims):
    high, low = split_value(values)
    axis = dims[0][0]
    left = jnp.concatenate([weights[0], weights[0], weights[1]], axis=axis)
    return lax.dot_general(
        left, jnp.concatenate([high, low, high], axis=0), (dims, ((), ())), preferred_element_type=f32
    )


def tensor_kernel(spread, to_special, out):
    lane = lax.broadcasted_iota(jnp.int32, (8, LANES), 1)
    half = lane < 64
    sign = jnp.where(half, 1.0, -1.0).astype(f32)
    limb_low = (lane & 4) == 0
    comp = lax.broadcasted_iota(jnp.int32, (16, LANES), 1) & 3

    def roll(value, shift):
        return pltpu.roll(value, shift % LANES, 1)

    rows = jnp.concatenate([to_special[pl.ds(limb, 8, stride=2), :] for limb in range(2)], axis=0)
    old = lax.broadcasted_iota(jnp.int32, (16, 16), 0)
    new = lax.broadcasted_iota(jnp.int32, (16, 16), 1)
    order = jnp.where(old == 2 * (new & 7) + (new >> 3), 1.0, 0.0).astype(bf16)
    extend = split_value(
        sum(
            lax.dot_general(part, order, (((1,), (0,)), ((), ())), preferred_element_type=f32)
            for part in split_value(rows)
        )
    )
    table = spread[pl.ds(1, GROUPS, stride=2 * COEF), :]
    shrink = split_value(jnp.concatenate([table[:, 16 * j : 16 * j + 16] for j in range(4)], axis=0))

    blocks = [spread[pl.ds(2 * c, GROUPS, stride=2 * COEF), :] for c in range(COEF)]
    spectra = []
    for _, (real, imag) in split_ring(list(zip(blocks[: COEF // 2], blocks[COEF // 2 :])), math.pi / 2):
        one = real - roll(imag, 64)
        two = imag + roll(real, 64)
        spectra.append((jnp.where(half, one, two), jnp.where(half, two, one)))

    def tensor(value):
        real, imag = value
        real_next, imag_next = (jnp.where(comp == 3, roll(part, 3), roll(part, -1)) for part in value)
        return real * real_next - imag * imag_next, real * imag_next + imag * real_next

    owns = []
    for place in range(COEF // 4):
        for part in range(2):
            one, two = spectra[2 * place][part], spectra[2 * place + 1][part]
            owns.append(
                jnp.concatenate(
                    [jnp.where(limb_low, one, roll(two, 4)), jnp.where(limb_low, roll(one, -4), two)], axis=0
                )
            )
    specials = mix(extend, jnp.concatenate(owns, axis=1), ((1,), (0,)))
    own_products, special_products = [], []
    for place in range(COEF // 4):
        start = place * 2 * LANES
        own_products += tensor(owns[2 * place : 2 * place + 2])
        special_products += tensor(
            (specials[:, start : start + LANES], specials[:, start + LANES : start + 2 * LANES])
        )
    products = jnp.concatenate(
        [jnp.concatenate(own_products, axis=1), jnp.concatenate(special_products, axis=1)], axis=0
    )
    scaled = mix(shrink, products, ((0,), (0,)))
    mixed = []
    for place in range(COEF // 4):
        parts = []
        for part in range(2):
            start = (2 * place + part) * LANES
            low, high = scaled[:8, start : start + LANES], scaled[8:, start : start + LANES]
            parts.append((jnp.where(limb_low, low, roll(high, 4)), jnp.where(limb_low, roll(low, -4), high)))
        mixed.append((parts[0][0], parts[1][0]))
        mixed.append((parts[0][1], parts[1][1]))

    share = 1.0 / (COEF * BLOCK)
    joined = []
    for (real, imag), theta in zip(mixed, root_angles(COEF // 2, math.pi / 2)):
        cosine = share + sign * (share * math.sin(theta))
        sine = -share * math.cos(theta)
        own_real, own_imag = real * cosine - imag * sine, imag * cosine + real * sine
        other_real, other_imag = roll(own_real, 64), roll(own_imag, 64)
        joined.append(
            (
                jnp.where(half, own_real + other_real, own_imag + other_imag),
                jnp.where(half, own_imag - other_imag, own_real - other_real),
            )
        )
    for c, (real, imag) in enumerate(join_ring(joined, math.pi / 2)):
        out[pl.ds(c, GROUPS, stride=COEF), :] = real
        out[pl.ds(c + COEF // 2, GROUPS, stride=COEF), :] = imag


def restore_kernel(gathered, wide_high, wide_low, twiddle, out):
    row = lax.broadcasted_iota(jnp.int32, (8, LANES), 0)
    middle = (row & 3) == 1
    values = split_value(jnp.concatenate([gathered[:LANES, :], gathered[LANES:, :]], axis=1))
    left = jnp.concatenate([values[0], values[1], values[0]], axis=0)
    right = jnp.concatenate([wide_high[...], wide_high[...], wide_low[...]], axis=0)
    both = lax.dot_general(left, right, (((0,), (0,)), ((), ())), preferred_element_type=f32)
    for pair in range(2):
        spun = both[pair * LANES : (pair + 1) * LANES]
        real = spun[:64, :LANES] + spun[64:, LANES:]
        imag = spun[64:, :LANES] - spun[:64, LANES:]
        turned = []
        for k0 in range(K0):
            cosine = twiddle[k0 : k0 + 1, :]
            sine = twiddle[K0 + k0 : K0 + k0 + 1, :]
            own_real, own_imag = real[k0 * 8 : k0 * 8 + 8], imag[k0 * 8 : k0 * 8 + 8]
            turned.append((own_real * cosine + own_imag * sine, own_imag * cosine - own_real * sine))
        halves = []
        for k0 in range(K0 // 2):
            one, two = turned[k0], turned[k0 + K0 // 2]
            halves.append(((one[0] + two[0], one[1] + two[1]), (one[0] - two[0], one[1] - two[1])))
        for u in range(U):
            total = None
            for k0 in range(K0 // 2):
                cosine, sine = turn(u, k0)
                real_part, imag_part = halves[k0][u % 2]
                term = real_part if u == 0 else real_part * cosine + imag_part * sine
                total = term if total is None else total + term
            total = jnp.where(middle, total + pltpu.roll(total, 6, 0), total)
            for limb in range(2):
                for part in range(3):
                    row = limb * 4 + part
                    out[limb, part, pair : pair + 1, u * LANES : (u + 1) * LANES] = total[row : row + 1]


def in_vmem():
    return pl.BlockSpec(memory_space=pltpu.VMEM)


def in_hbm():
    return pl.BlockSpec(memory_space=pltpu.HBM)


def kept_far(*arrays):
    return [pltpu.with_memory_space_constraint(array, pltpu.HBM) for array in arrays]


def per_device(first_cipher, second_cipher, to_special, keep_table, scale_table):
    (wide_high, wide_low), twiddle = turn_tables()
    wide_high, wide_low, twiddle = jnp.asarray(wide_high), jnp.asarray(wide_low), jnp.asarray(twiddle)
    params = pltpu.CompilerParams(vmem_limit_bytes=32 * 1024 * 1024)
    spectra = pl.pallas_call(
        evaluate_kernel,
        out_shape=jax.ShapeDtypeStruct((2 * ROOTS, LANES), f32),
        in_specs=[in_hbm()] * 7,
        out_specs=in_vmem(),
        scratch_shapes=[
            pltpu.VMEM(first_cipher.shape, f32),
            pltpu.VMEM(second_cipher.shape, f32),
            pltpu.SMEM((2, 16), f32),
            pltpu.SMEM((2, 16), f32),
            pltpu.VMEM(wide_high.shape, bf16),
            pltpu.VMEM(wide_low.shape, bf16),
            pltpu.VMEM(twiddle.shape, f32),
            pltpu.VMEM((2 * U * 8 + 16, LANES), f32),
            pltpu.SemaphoreType.DMA((7,)),
        ],
        compiler_params=params,
        name="evaluate",
    )(*kept_far(first_cipher, second_cipher, keep_table.T, scale_table.T, wide_high, wide_low, twiddle))
    spread = lax.all_to_all(spectra.reshape(ROOTS, 2, LANES), ("limb", "coef"), 0, 0)
    scaled = pl.pallas_call(
        tensor_kernel,
        out_shape=jax.ShapeDtypeStruct((ROOTS, LANES), f32),
        in_specs=[in_vmem()] * 2,
        out_specs=in_vmem(),
        compiler_params=params,
        name="tensor",
    )(spread.reshape(2 * ROOTS, LANES), to_special)
    gathered = lax.all_to_all(scaled.reshape(ROOTS, 1, LANES), ("limb", "coef"), 0, 0)
    product = pl.pallas_call(
        restore_kernel,
        out_shape=jax.ShapeDtypeStruct((2, 3, 2, BLOCK), f32),
        in_specs=[in_vmem()] * 4,
        out_specs=in_vmem(),
        compiler_params=params,
        name="restore",
    )(gathered.reshape(ROOTS, LANES), wide_high, wide_low, twiddle)
    return product.transpose(0, 2, 1, 3)


def solution(mesh):
    return jax.shard_map(
        per_device,
        mesh=mesh,
        in_specs=(
            P("limb", None, None, "coef"),
            P("limb", None, None, "coef"),
            P(),
            P(None, "limb"),
            P(None, "limb"),
        ),
        out_specs=P("limb", None, None, "coef"),
        check_vma=False,
    )
```

```python
import math

import jax
import jax.numpy as jnp
import ml_dtypes
import numpy as np
from jax import lax
from jax.experimental import pallas as pl
from jax.experimental.pallas import tpu as pltpu
from jax.sharding import PartitionSpec as P

LANES = 128
U = 8
K0 = 8
BLOCK = U * LANES
COEF = 32
GROUPS = 8
ROOTS = 2 * LANES
f32 = jnp.float32
bf16 = jnp.bfloat16


def split_constant(values):
    high = values.astype(np.float32).astype(ml_dtypes.bfloat16)
    low = (values - high.astype(np.float64)).astype(ml_dtypes.bfloat16)
    return high, low


def turn_tables():
    index = np.arange(LANES)
    angle = 2 * np.pi * (index[:, None] * index[None, :] % LANES) / LANES
    wide = np.concatenate([np.cos(angle), np.sin(angle)], axis=1)
    v = np.arange(LANES)[None, :]
    k0 = np.arange(K0)[:, None]
    phase = np.pi * v * (4 * k0 + 1) / 2048
    twiddle = np.concatenate([np.cos(phase), np.sin(phase)], axis=0)
    return split_constant(wide), twiddle.astype(np.float32)


def split_value(values):
    high = values.astype(bf16)
    low = (values - high.astype(f32)).astype(bf16)
    return high, low


def dot3(left, right, dims):
    def one(a, b):
        return lax.dot_general(a, b, (dims, ((), ())), preferred_element_type=f32)

    return one(left[0], right[0]) + (one(left[0], right[1]) + one(left[1], right[0]))


def turn(u, k0):
    angle = math.pi * u * (4 * k0 + 1) / 16
    return math.cos(angle), math.sin(angle)


def evaluate_kernel(
    first_far, second_far, keep_far, scale_far, high_far, low_far, twiddle_far,
    out,
    first, second, keep, scale, wide_high, wide_low, twiddle, held, sems,
):
    copies = [
        pltpu.make_async_copy(far, near, sems.at[place])
        for place, (far, near) in enumerate(
            (
                (first_far, first),
                (second_far, second),
                (twiddle_far, twiddle),
                (high_far, wide_high),
                (low_far, wide_low),
                (keep_far, keep),
                (scale_far, scale),
            )
        )
    ]
    for copy in copies:
        copy.start()
    copies[0].wait()
    copies[1].wait()
    for pair in range(2):
        for u in range(U):
            base = (pair * U + u) * 8
            for limb in range(2):
                for cipher, ref in enumerate((first, second)):
                    held[pl.ds(base + limb * 4 + cipher, 2, stride=2), :] = ref[
                        limb, pair, :, u * LANES : (u + 1) * LANES
                    ]
    copies[2].wait()
    copies[5].wait()
    copies[6].wait()
    lane = lax.broadcasted_iota(jnp.int32, (8, LANES), 1)
    table = jnp.zeros((8, LANES), f32)
    for i in range(16):
        for limb in range(2):
            place = limb * 16 + (i % 2) * 8 + i // 2
            table = jnp.where(lane == place, keep[limb, i], table)
            table = jnp.where(lane == 32 + place, scale[limb, i], table)
    for tile in range(ROOTS // 8):
        out[pl.ds(tile * 16 + 1, 8, stride=2), :] = table
    blocks = []
    for pair in range(2):
        parts = [held[(pair * U + u) * 8 : (pair * U + u + 1) * 8, :] for u in range(U)]
        spun = [None] * K0
        for k0 in range(K0 // 2):
            sums = []
            for start in (0, 1):
                real = imag = None
                for u in range(start, U, 2):
                    cosine, sine = turn(u, k0)
                    term_real = parts[u] if u == 0 else parts[u] * cosine
                    real = term_real if real is None else real + term_real
                    if u:
                        term_imag = parts[u] * sine
                        imag = term_imag if imag is None else imag + term_imag
                sums.append((real, imag))
            (even_real, even_imag), (odd_real, odd_imag) = sums
            spun[k0] = (even_real + odd_real, even_imag + odd_imag)
            spun[k0 + K0 // 2] = (even_real - odd_real, even_imag - odd_imag)
        reals, imags = [], []
        for k0 in range(K0):
            cosine = twiddle[k0 : k0 + 1, :]
            sine = twiddle[K0 + k0 : K0 + k0 + 1, :]
            real, imag = spun[k0]
            reals.append(real * cosine - imag * sine)
            imags.append(real * sine + imag * cosine)
        real = jnp.concatenate(reals, axis=0)
        imag = jnp.concatenate(imags, axis=0)
        blocks.append(jnp.concatenate([real, -imag], axis=1))
        blocks.append(jnp.concatenate([imag, real], axis=1))
    rows = jnp.concatenate(blocks, axis=0)
    copies[3].wait()
    copies[4].wait()
    left = jnp.concatenate([wide_high[...], wide_high[...], wide_low[...]], axis=1)
    halves = []
    for pair in range(2):
        high, low = split_value(jnp.concatenate(blocks[2 * pair : 2 * pair + 2], axis=0))
        halves.append(
            lax.dot_general(
                left, jnp.concatenate([high, low, high], axis=1), (((1,), (1,)), ((), ())), preferred_element_type=f32
            )
        )
    spectrum = jnp.concatenate(halves, axis=1)
    for pair in range(2):
        out[pl.ds(pair * 256, LANES, stride=2), :] = spectrum[:, pair * LANES : (pair + 1) * LANES]


def complex_scale(value, cosine, sine):
    real, imag = value
    if abs(cosine) < 1e-9:
        return (-imag, real) if sine > 0 else (imag, -real)
    if abs(abs(cosine) - abs(sine)) < 1e-9:
        if cosine * sine > 0:
            return (real - imag) * cosine, (real + imag) * cosine
        return (real + imag) * cosine, (imag - real) * cosine
    return real * cosine - imag * sine, real * sine + imag * cosine


def split_ring(values, theta):
    if len(values) == 1:
        return [(theta, values[0])]
    half = len(values) // 2
    cosine, sine = math.cos(theta / 2), math.sin(theta / 2)
    left, right = [], []
    for low, high in zip(values[:half], values[half:]):
        moved = complex_scale(high, cosine, sine)
        left.append((low[0] + moved[0], low[1] + moved[1]))
        right.append((low[0] - moved[0], low[1] - moved[1]))
    return split_ring(left, theta / 2) + split_ring(right, theta / 2 + math.pi)


def join_ring(values, theta):
    if len(values) == 1:
        return values
    half = len(values) // 2
    left = join_ring(values[:half], theta / 2)
    right = join_ring(values[half:], theta / 2 + math.pi)
    cosine, sine = math.cos(theta / 2), math.sin(theta / 2)
    low, high = [], []
    for one, two in zip(left, right):
        low.append((one[0] + two[0], one[1] + two[1]))
        high.append(complex_scale((one[0] - two[0], one[1] - two[1]), cosine, -sine))
    return low + high


def root_angles(count, theta):
    if count == 1:
        return [theta]
    return root_angles(count // 2, theta / 2) + root_angles(count // 2, theta / 2 + math.pi)


def mix(weights, values, dims):
    high, low = split_value(values)
    axis = dims[0][0]
    left = jnp.concatenate([weights[0], weights[0], weights[1]], axis=axis)
    return lax.dot_general(
        left, jnp.concatenate([high, low, high], axis=0), (dims, ((), ())), preferred_element_type=f32
    )


def tensor_kernel(spread, to_special, out):
    lane = lax.broadcasted_iota(jnp.int32, (8, LANES), 1)
    half = lane < 64
    sign = jnp.where(half, 1.0, -1.0).astype(f32)
    limb_low = (lane & 4) == 0
    comp = lax.broadcasted_iota(jnp.int32, (16, LANES), 1) & 3

    def roll(value, shift):
        return pltpu.roll(value, shift % LANES, 1)

    rows = jnp.concatenate([to_special[pl.ds(limb, 8, stride=2), :] for limb in range(2)], axis=0)
    old = lax.broadcasted_iota(jnp.int32, (16, 16), 0)
    new = lax.broadcasted_iota(jnp.int32, (16, 16), 1)
    order = jnp.where(old == 2 * (new & 7) + (new >> 3), 1.0, 0.0).astype(bf16)
    extend = split_value(
        sum(
            lax.dot_general(part, order, (((1,), (0,)), ((), ())), preferred_element_type=f32)
            for part in split_value(rows)
        )
    )
    table = spread[pl.ds(1, GROUPS, stride=2 * COEF), :]
    shrink = split_value(jnp.concatenate([table[:, 16 * j : 16 * j + 16] for j in range(4)], axis=0))

    blocks = [spread[pl.ds(2 * c, GROUPS, stride=2 * COEF), :] for c in range(COEF)]
    spectra = []
    for _, (real, imag) in split_ring(list(zip(blocks[: COEF // 2], blocks[COEF // 2 :])), math.pi / 2):
        one = real - roll(imag, 64)
        two = imag + roll(real, 64)
        spectra.append((jnp.where(half, one, two), jnp.where(half, two, one)))

    def tensor(value):
        real, imag = value
        real_next, imag_next = (jnp.where(comp == 3, roll(part, 3), roll(part, -1)) for part in value)
        return real * real_next - imag * imag_next, real * imag_next + imag * real_next

    owns = []
    for place in range(COEF // 4):
        for part in range(2):
            one, two = spectra[2 * place][part], spectra[2 * place + 1][part]
            owns.append(
                jnp.concatenate(
                    [jnp.where(limb_low, one, roll(two, 4)), jnp.where(limb_low, roll(one, -4), two)], axis=0
                )
            )
    specials = mix(extend, jnp.concatenate(owns, axis=1), ((1,), (0,)))
    own_products, special_products = [], []
    for place in range(COEF // 4):
        start = place * 2 * LANES
        own_products += tensor(owns[2 * place : 2 * place + 2])
        special_products += tensor(
            (specials[:, start : start + LANES], specials[:, start + LANES : start + 2 * LANES])
        )
    products = jnp.concatenate(
        [jnp.concatenate(own_products, axis=1), jnp.concatenate(special_products, axis=1)], axis=0
    )
    scaled = mix(shrink, products, ((0,), (0,)))
    mixed = []
    for place in range(COEF // 4):
        parts = []
        for part in range(2):
            start = (2 * place + part) * LANES
            low, high = scaled[:8, start : start + LANES], scaled[8:, start : start + LANES]
            parts.append((jnp.where(limb_low, low, roll(high, 4)), jnp.where(limb_low, roll(low, -4), high)))
        mixed.append((parts[0][0], parts[1][0]))
        mixed.append((parts[0][1], parts[1][1]))

    share = 1.0 / (COEF * BLOCK)
    joined = []
    for (real, imag), theta in zip(mixed, root_angles(COEF // 2, math.pi / 2)):
        cosine = share + sign * (share * math.sin(theta))
        sine = -share * math.cos(theta)
        own_real, own_imag = real * cosine - imag * sine, imag * cosine + real * sine
        other_real, other_imag = roll(own_real, 64), roll(own_imag, 64)
        joined.append(
            (
                jnp.where(half, own_real + other_real, own_imag + other_imag),
                jnp.where(half, own_imag - other_imag, own_real - other_real),
            )
        )
    for c, (real, imag) in enumerate(join_ring(joined, math.pi / 2)):
        out[pl.ds(c, GROUPS, stride=COEF), :] = real
        out[pl.ds(c + COEF // 2, GROUPS, stride=COEF), :] = imag


def restore_kernel(gathered, wide_high, wide_low, twiddle, out):
    row = lax.broadcasted_iota(jnp.int32, (8, LANES), 0)
    middle = (row & 3) == 1
    values = split_value(jnp.concatenate([gathered[:LANES, :], gathered[LANES:, :]], axis=1))
    left = jnp.concatenate([values[0], values[1], values[0]], axis=0)
    right = jnp.concatenate([wide_high[...], wide_high[...], wide_low[...]], axis=0)
    both = lax.dot_general(left, right, (((0,), (0,)), ((), ())), preferred_element_type=f32)
    for pair in range(2):
        spun = both[pair * LANES : (pair + 1) * LANES]
        real = spun[:64, :LANES] + spun[64:, LANES:]
        imag = spun[64:, :LANES] - spun[:64, LANES:]
        turned = []
        for k0 in range(K0):
            cosine = twiddle[k0 : k0 + 1, :]
            sine = twiddle[K0 + k0 : K0 + k0 + 1, :]
            own_real, own_imag = real[k0 * 8 : k0 * 8 + 8], imag[k0 * 8 : k0 * 8 + 8]
            turned.append((own_real * cosine + own_imag * sine, own_imag * cosine - own_real * sine))
        halves = []
        for k0 in range(K0 // 2):
            one, two = turned[k0], turned[k0 + K0 // 2]
            halves.append(((one[0] + two[0], one[1] + two[1]), (one[0] - two[0], one[1] - two[1])))
        quarters = []
        for k0 in range(K0 // 4):
            (even, odd), (even_far, odd_far) = halves[k0], halves[k0 + 2]
            quarters.append(
                (
                    (even[0] + even_far[0], even[1] + even_far[1]),
                    (odd[0] + odd_far[1], odd[1] - odd_far[0]),
                    (even[0] - even_far[0], even[1] - even_far[1]),
                    (odd[0] - odd_far[1], odd[1] + odd_far[0]),
                )
            )
        for u in range(U):
            total = None
            for k0 in range(K0 // 4):
                cosine, sine = turn(u, k0)
                real_part, imag_part = quarters[k0][u % 4]
                term = real_part if u == 0 else real_part * cosine + imag_part * sine
                total = term if total is None else total + term
            total = jnp.where(middle, total + pltpu.roll(total, 6, 0), total)
            for limb in range(2):
                for part in range(3):
                    row = limb * 4 + part
                    out[limb, part, pair : pair + 1, u * LANES : (u + 1) * LANES] = total[row : row + 1]


def in_vmem():
    return pl.BlockSpec(memory_space=pltpu.VMEM)


def in_hbm():
    return pl.BlockSpec(memory_space=pltpu.HBM)


def kept_far(*arrays):
    return [pltpu.with_memory_space_constraint(array, pltpu.HBM) for array in arrays]


def per_device(first_cipher, second_cipher, to_special, keep_table, scale_table):
    (wide_high, wide_low), twiddle = turn_tables()
    wide_high, wide_low, twiddle = jnp.asarray(wide_high), jnp.asarray(wide_low), jnp.asarray(twiddle)
    params = pltpu.CompilerParams(vmem_limit_bytes=32 * 1024 * 1024)
    spectra = pl.pallas_call(
        evaluate_kernel,
        out_shape=jax.ShapeDtypeStruct((2 * ROOTS, LANES), f32),
        in_specs=[in_hbm()] * 7,
        out_specs=in_vmem(),
        scratch_shapes=[
            pltpu.VMEM(first_cipher.shape, f32),
            pltpu.VMEM(second_cipher.shape, f32),
            pltpu.SMEM((2, 16), f32),
            pltpu.SMEM((2, 16), f32),
            pltpu.VMEM(wide_high.shape, bf16),
            pltpu.VMEM(wide_low.shape, bf16),
            pltpu.VMEM(twiddle.shape, f32),
            pltpu.VMEM((2 * U * 8 + 16, LANES), f32),
            pltpu.SemaphoreType.DMA((7,)),
        ],
        compiler_params=params,
        name="evaluate",
    )(*kept_far(first_cipher, second_cipher, keep_table.T, scale_table.T, wide_high, wide_low, twiddle))
    spread = lax.all_to_all(spectra.reshape(ROOTS, 2, LANES), ("limb", "coef"), 0, 0)
    scaled = pl.pallas_call(
        tensor_kernel,
        out_shape=jax.ShapeDtypeStruct((ROOTS, LANES), f32),
        in_specs=[in_vmem()] * 2,
        out_specs=in_vmem(),
        compiler_params=params,
        name="tensor",
    )(spread.reshape(2 * ROOTS, LANES), to_special)
    gathered = lax.all_to_all(scaled.reshape(ROOTS, 1, LANES), ("limb", "coef"), 0, 0)
    product = pl.pallas_call(
        restore_kernel,
        out_shape=jax.ShapeDtypeStruct((2, 3, 2, BLOCK), f32),
        in_specs=[in_vmem()] * 4,
        out_specs=in_vmem(),
        compiler_params=params,
        name="restore",
    )(gathered.reshape(ROOTS, LANES), wide_high, wide_low, twiddle)
    return product.transpose(0, 2, 1, 3)


def solution(mesh):
    return jax.shard_map(
        per_device,
        mesh=mesh,
        in_specs=(
            P("limb", None, None, "coef"),
            P("limb", None, None, "coef"),
            P(),
            P(None, "limb"),
            P(None, "limb"),
        ),
        out_specs=P("limb", None, None, "coef"),
        check_vma=False,
    )
```

```python
import math

import jax
import jax.numpy as jnp
import ml_dtypes
import numpy as np
from jax import lax
from jax.experimental import pallas as pl
from jax.experimental.pallas import tpu as pltpu
from jax.sharding import PartitionSpec as P

LANES = 128
U = 8
K0 = 8
BLOCK = U * LANES
COEF = 32
GROUPS = 8
ROOTS = 2 * LANES
f32 = jnp.float32
bf16 = jnp.bfloat16


def split_constant(values):
    high = values.astype(np.float32).astype(ml_dtypes.bfloat16)
    low = (values - high.astype(np.float64)).astype(ml_dtypes.bfloat16)
    return high, low


def turn_tables():
    index = np.arange(LANES)
    angle = 2 * np.pi * (index[:, None] * index[None, :] % LANES) / LANES
    wide = np.concatenate([np.cos(angle), np.sin(angle)], axis=1)
    v = np.arange(LANES)[None, :]
    k0 = np.arange(K0)[:, None]
    phase = np.pi * v * (4 * k0 + 1) / 2048
    twiddle = np.concatenate([np.cos(phase), np.sin(phase)], axis=0)
    return split_constant(wide), twiddle.astype(np.float32)


def split_value(values):
    high = values.astype(bf16)
    low = (values - high.astype(f32)).astype(bf16)
    return high, low


def dot3(left, right, dims):
    def one(a, b):
        return lax.dot_general(a, b, (dims, ((), ())), preferred_element_type=f32)

    return one(left[0], right[0]) + (one(left[0], right[1]) + one(left[1], right[0]))


def turn(u, k0):
    angle = math.pi * u * (4 * k0 + 1) / 16
    return math.cos(angle), math.sin(angle)


def evaluate_kernel(
    first_far, second_far, keep_far, scale_far, high_far, low_far, twiddle_far,
    out,
    first, second, keep, scale, wide_high, wide_low, twiddle, held, sems,
):
    copies = [
        pltpu.make_async_copy(far, near, sems.at[place])
        for place, (far, near) in enumerate(
            (
                (first_far, first),
                (second_far, second),
                (twiddle_far, twiddle),
                (high_far, wide_high),
                (low_far, wide_low),
                (keep_far, keep),
                (scale_far, scale),
            )
        )
    ]
    for copy in copies:
        copy.start()
    copies[0].wait()
    copies[1].wait()
    for pair in range(2):
        for u in range(U):
            base = (pair * U + u) * 8
            for limb in range(2):
                for cipher, ref in enumerate((first, second)):
                    held[pl.ds(base + limb * 4 + cipher, 2, stride=2), :] = ref[
                        limb, pair, :, u * LANES : (u + 1) * LANES
                    ]
    copies[2].wait()
    copies[5].wait()
    copies[6].wait()
    lane = lax.broadcasted_iota(jnp.int32, (8, LANES), 1)
    table = jnp.zeros((8, LANES), f32)
    for i in range(16):
        for limb in range(2):
            place = limb * 16 + (i % 2) * 8 + i // 2
            table = jnp.where(lane == place, keep[limb, i], table)
            table = jnp.where(lane == 32 + place, scale[limb, i], table)
    for tile in range(ROOTS // 8):
        out[pl.ds(tile * 16 + 1, 8, stride=2), :] = table
    blocks = []
    for pair in range(2):
        parts = [held[(pair * U + u) * 8 : (pair * U + u + 1) * 8, :] for u in range(U)]
        spun = [None] * K0
        for k0 in range(K0 // 4):
            sums = []
            for start in range(4):
                real = imag = None
                for u in range(start, U, 4):
                    cosine, sine = turn(u, k0)
                    term_real = parts[u] if u == 0 else parts[u] * cosine
                    real = term_real if real is None else real + term_real
                    if u:
                        term_imag = parts[u] * sine
                        imag = term_imag if imag is None else imag + term_imag
                sums.append((real, imag))
            zero, one, two, three = sums
            even = (zero[0] + two[0], zero[1] + two[1])
            odd = (one[0] + three[0], one[1] + three[1])
            even_gap = (zero[0] - two[0], zero[1] - two[1])
            odd_gap = (three[1] - one[1], one[0] - three[0])
            spun[k0] = (even[0] + odd[0], even[1] + odd[1])
            spun[k0 + 2] = (even_gap[0] + odd_gap[0], even_gap[1] + odd_gap[1])
            spun[k0 + 4] = (even[0] - odd[0], even[1] - odd[1])
            spun[k0 + 6] = (even_gap[0] - odd_gap[0], even_gap[1] - odd_gap[1])
        reals, imags = [], []
        for k0 in range(K0):
            cosine = twiddle[k0 : k0 + 1, :]
            sine = twiddle[K0 + k0 : K0 + k0 + 1, :]
            real, imag = spun[k0]
            reals.append(real * cosine - imag * sine)
            imags.append(real * sine + imag * cosine)
        real = jnp.concatenate(reals, axis=0)
        imag = jnp.concatenate(imags, axis=0)
        blocks.append(jnp.concatenate([real, -imag], axis=1))
        blocks.append(jnp.concatenate([imag, real], axis=1))
    rows = jnp.concatenate(blocks, axis=0)
    copies[3].wait()
    copies[4].wait()
    left = jnp.concatenate([wide_high[...], wide_high[...], wide_low[...]], axis=1)
    halves = []
    for pair in range(2):
        high, low = split_value(jnp.concatenate(blocks[2 * pair : 2 * pair + 2], axis=0))
        halves.append(
            lax.dot_general(
                left, jnp.concatenate([high, low, high], axis=1), (((1,), (1,)), ((), ())), preferred_element_type=f32
            )
        )
    spectrum = jnp.concatenate(halves, axis=1)
    for pair in range(2):
        out[pl.ds(pair * 256, LANES, stride=2), :] = spectrum[:, pair * LANES : (pair + 1) * LANES]


def complex_scale(value, cosine, sine):
    real, imag = value
    if abs(cosine) < 1e-9:
        return (-imag, real) if sine > 0 else (imag, -real)
    if abs(abs(cosine) - abs(sine)) < 1e-9:
        if cosine * sine > 0:
            return (real - imag) * cosine, (real + imag) * cosine
        return (real + imag) * cosine, (imag - real) * cosine
    return real * cosine - imag * sine, real * sine + imag * cosine


def split_ring(values, theta):
    if len(values) == 1:
        return [(theta, values[0])]
    half = len(values) // 2
    cosine, sine = math.cos(theta / 2), math.sin(theta / 2)
    left, right = [], []
    for low, high in zip(values[:half], values[half:]):
        moved = complex_scale(high, cosine, sine)
        left.append((low[0] + moved[0], low[1] + moved[1]))
        right.append((low[0] - moved[0], low[1] - moved[1]))
    return split_ring(left, theta / 2) + split_ring(right, theta / 2 + math.pi)


def join_ring(values, theta):
    if len(values) == 1:
        return values
    half = len(values) // 2
    left = join_ring(values[:half], theta / 2)
    right = join_ring(values[half:], theta / 2 + math.pi)
    cosine, sine = math.cos(theta / 2), math.sin(theta / 2)
    low, high = [], []
    for one, two in zip(left, right):
        low.append((one[0] + two[0], one[1] + two[1]))
        high.append(complex_scale((one[0] - two[0], one[1] - two[1]), cosine, -sine))
    return low + high


def root_angles(count, theta):
    if count == 1:
        return [theta]
    return root_angles(count // 2, theta / 2) + root_angles(count // 2, theta / 2 + math.pi)


def mix(weights, values, dims):
    high, low = split_value(values)
    axis = dims[0][0]
    left = jnp.concatenate([weights[0], weights[0], weights[1]], axis=axis)
    return lax.dot_general(
        left, jnp.concatenate([high, low, high], axis=0), (dims, ((), ())), preferred_element_type=f32
    )


def tensor_kernel(spread, to_special, out):
    lane = lax.broadcasted_iota(jnp.int32, (8, LANES), 1)
    half = lane < 64
    sign = jnp.where(half, 1.0, -1.0).astype(f32)
    limb_low = (lane & 4) == 0
    comp = lax.broadcasted_iota(jnp.int32, (16, LANES), 1) & 3

    def roll(value, shift):
        return pltpu.roll(value, shift % LANES, 1)

    rows = jnp.concatenate([to_special[pl.ds(limb, 8, stride=2), :] for limb in range(2)], axis=0)
    old = lax.broadcasted_iota(jnp.int32, (16, 16), 0)
    new = lax.broadcasted_iota(jnp.int32, (16, 16), 1)
    order = jnp.where(old == 2 * (new & 7) + (new >> 3), 1.0, 0.0).astype(bf16)
    extend = split_value(
        sum(
            lax.dot_general(part, order, (((1,), (0,)), ((), ())), preferred_element_type=f32)
            for part in split_value(rows)
        )
    )
    table = spread[pl.ds(1, GROUPS, stride=2 * COEF), :]
    shrink = split_value(jnp.concatenate([table[:, 16 * j : 16 * j + 16] for j in range(4)], axis=0))

    blocks = [spread[pl.ds(2 * c, GROUPS, stride=2 * COEF), :] for c in range(COEF)]
    spectra = []
    for _, (real, imag) in split_ring(list(zip(blocks[: COEF // 2], blocks[COEF // 2 :])), math.pi / 2):
        one = real - roll(imag, 64)
        two = imag + roll(real, 64)
        spectra.append((jnp.where(half, one, two), jnp.where(half, two, one)))

    def tensor(value):
        real, imag = value
        real_next, imag_next = (jnp.where(comp == 3, roll(part, 3), roll(part, -1)) for part in value)
        return real * real_next - imag * imag_next, real * imag_next + imag * real_next

    owns = []
    for place in range(COEF // 4):
        for part in range(2):
            one, two = spectra[2 * place][part], spectra[2 * place + 1][part]
            owns.append(
                jnp.concatenate(
                    [jnp.where(limb_low, one, roll(two, 4)), jnp.where(limb_low, roll(one, -4), two)], axis=0
                )
            )
    specials = mix(extend, jnp.concatenate(owns, axis=1), ((1,), (0,)))
    own_products, special_products = [], []
    for place in range(COEF // 4):
        start = place * 2 * LANES
        own_products += tensor(owns[2 * place : 2 * place + 2])
        special_products += tensor(
            (specials[:, start : start + LANES], specials[:, start + LANES : start + 2 * LANES])
        )
    products = jnp.concatenate(
        [jnp.concatenate(own_products, axis=1), jnp.concatenate(special_products, axis=1)], axis=0
    )
    scaled = mix(shrink, products, ((0,), (0,)))
    mixed = []
    for place in range(COEF // 4):
        parts = []
        for part in range(2):
            start = (2 * place + part) * LANES
            low, high = scaled[:8, start : start + LANES], scaled[8:, start : start + LANES]
            parts.append((jnp.where(limb_low, low, roll(high, 4)), jnp.where(limb_low, roll(low, -4), high)))
        mixed.append((parts[0][0], parts[1][0]))
        mixed.append((parts[0][1], parts[1][1]))

    share = 1.0 / (COEF * BLOCK)
    joined = []
    for (real, imag), theta in zip(mixed, root_angles(COEF // 2, math.pi / 2)):
        cosine = share + sign * (share * math.sin(theta))
        sine = -share * math.cos(theta)
        own_real, own_imag = real * cosine - imag * sine, imag * cosine + real * sine
        other_real, other_imag = roll(own_real, 64), roll(own_imag, 64)
        joined.append(
            (
                jnp.where(half, own_real + other_real, own_imag + other_imag),
                jnp.where(half, own_imag - other_imag, own_real - other_real),
            )
        )
    for c, (real, imag) in enumerate(join_ring(joined, math.pi / 2)):
        out[pl.ds(c, GROUPS, stride=COEF), :] = real
        out[pl.ds(c + COEF // 2, GROUPS, stride=COEF), :] = imag


def restore_kernel(gathered, wide_high, wide_low, twiddle, out):
    row = lax.broadcasted_iota(jnp.int32, (8, LANES), 0)
    middle = (row & 3) == 1
    values = split_value(jnp.concatenate([gathered[:LANES, :], gathered[LANES:, :]], axis=1))
    left = jnp.concatenate([values[0], values[1], values[0]], axis=0)
    right = jnp.concatenate([wide_high[...], wide_high[...], wide_low[...]], axis=0)
    both = lax.dot_general(left, right, (((0,), (0,)), ((), ())), preferred_element_type=f32)
    for pair in range(2):
        spun = both[pair * LANES : (pair + 1) * LANES]
        real = spun[:64, :LANES] + spun[64:, LANES:]
        imag = spun[64:, :LANES] - spun[:64, LANES:]
        turned = []
        for k0 in range(K0):
            cosine = twiddle[k0 : k0 + 1, :]
            sine = twiddle[K0 + k0 : K0 + k0 + 1, :]
            own_real, own_imag = real[k0 * 8 : k0 * 8 + 8], imag[k0 * 8 : k0 * 8 + 8]
            turned.append((own_real * cosine + own_imag * sine, own_imag * cosine - own_real * sine))
        halves = []
        for k0 in range(K0 // 2):
            one, two = turned[k0], turned[k0 + K0 // 2]
            halves.append(((one[0] + two[0], one[1] + two[1]), (one[0] - two[0], one[1] - two[1])))
        quarters = []
        for k0 in range(K0 // 4):
            (even, odd), (even_far, odd_far) = halves[k0], halves[k0 + 2]
            quarters.append(
                (
                    (even[0] + even_far[0], even[1] + even_far[1]),
                    (odd[0] + odd_far[1], odd[1] - odd_far[0]),
                    (even[0] - even_far[0], even[1] - even_far[1]),
                    (odd[0] - odd_far[1], odd[1] + odd_far[0]),
                )
            )
        for u in range(U):
            total = None
            for k0 in range(K0 // 4):
                cosine, sine = turn(u, k0)
                real_part, imag_part = quarters[k0][u % 4]
                term = real_part if u == 0 else real_part * cosine + imag_part * sine
                total = term if total is None else total + term
            total = jnp.where(middle, total + pltpu.roll(total, 6, 0), total)
            for limb in range(2):
                for part in range(3):
                    row = limb * 4 + part
                    out[limb, part, pair : pair + 1, u * LANES : (u + 1) * LANES] = total[row : row + 1]


def in_vmem():
    return pl.BlockSpec(memory_space=pltpu.VMEM)


def in_hbm():
    return pl.BlockSpec(memory_space=pltpu.HBM)


def kept_far(*arrays):
    return [pltpu.with_memory_space_constraint(array, pltpu.HBM) for array in arrays]


def per_device(first_cipher, second_cipher, to_special, keep_table, scale_table):
    (wide_high, wide_low), twiddle = turn_tables()
    wide_high, wide_low, twiddle = jnp.asarray(wide_high), jnp.asarray(wide_low), jnp.asarray(twiddle)
    params = pltpu.CompilerParams(vmem_limit_bytes=32 * 1024 * 1024)
    spectra = pl.pallas_call(
        evaluate_kernel,
        out_shape=jax.ShapeDtypeStruct((2 * ROOTS, LANES), f32),
        in_specs=[in_hbm()] * 7,
        out_specs=in_vmem(),
        scratch_shapes=[
            pltpu.VMEM(first_cipher.shape, f32),
            pltpu.VMEM(second_cipher.shape, f32),
            pltpu.SMEM((2, 16), f32),
            pltpu.SMEM((2, 16), f32),
            pltpu.VMEM(wide_high.shape, bf16),
            pltpu.VMEM(wide_low.shape, bf16),
            pltpu.VMEM(twiddle.shape, f32),
            pltpu.VMEM((2 * U * 8 + 16, LANES), f32),
            pltpu.SemaphoreType.DMA((7,)),
        ],
        compiler_params=params,
        name="evaluate",
    )(*kept_far(first_cipher, second_cipher, keep_table.T, scale_table.T, wide_high, wide_low, twiddle))
    spread = lax.all_to_all(spectra.reshape(ROOTS, 2, LANES), ("limb", "coef"), 0, 0)
    scaled = pl.pallas_call(
        tensor_kernel,
        out_shape=jax.ShapeDtypeStruct((ROOTS, LANES), f32),
        in_specs=[in_vmem()] * 2,
        out_specs=in_vmem(),
        compiler_params=params,
        name="tensor",
    )(spread.reshape(2 * ROOTS, LANES), to_special)
    gathered = lax.all_to_all(scaled.reshape(ROOTS, 1, LANES), ("limb", "coef"), 0, 0)
    product = pl.pallas_call(
        restore_kernel,
        out_shape=jax.ShapeDtypeStruct((2, 3, 2, BLOCK), f32),
        in_specs=[in_vmem()] * 4,
        out_specs=in_vmem(),
        compiler_params=params,
        name="restore",
    )(gathered.reshape(ROOTS, LANES), wide_high, wide_low, twiddle)
    return product.transpose(0, 2, 1, 3)


def solution(mesh):
    return jax.shard_map(
        per_device,
        mesh=mesh,
        in_specs=(
            P("limb", None, None, "coef"),
            P("limb", None, None, "coef"),
            P(),
            P(None, "limb"),
            P(None, "limb"),
        ),
        out_specs=P("limb", None, None, "coef"),
        check_vma=False,
    )
```

```python
import math

import jax
import jax.numpy as jnp
import ml_dtypes
import numpy as np
from jax import lax
from jax.experimental import pallas as pl
from jax.experimental.pallas import tpu as pltpu
from jax.sharding import PartitionSpec as P

LANES = 128
U = 8
K0 = 8
BLOCK = U * LANES
COEF = 32
GROUPS = 8
ROOTS = 2 * LANES
f32 = jnp.float32
bf16 = jnp.bfloat16


def split_constant(values):
    high = values.astype(np.float32).astype(ml_dtypes.bfloat16)
    low = (values - high.astype(np.float64)).astype(ml_dtypes.bfloat16)
    return high, low


def turn_tables():
    index = np.arange(LANES)
    angle = 2 * np.pi * (index[:, None] * index[None, :] % LANES) / LANES
    wide = np.concatenate([np.cos(angle), np.sin(angle)], axis=1)
    v = np.arange(LANES)[None, :]
    k0 = np.arange(K0)[:, None]
    phase = np.pi * v * (4 * k0 + 1) / 2048
    twiddle = np.concatenate([np.cos(phase), np.sin(phase)], axis=0)
    return split_constant(wide), twiddle.astype(np.float32)


def split_value(values):
    high = values.astype(bf16)
    low = (values - high.astype(f32)).astype(bf16)
    return high, low


def dot3(left, right, dims):
    def one(a, b):
        return lax.dot_general(a, b, (dims, ((), ())), preferred_element_type=f32)

    return one(left[0], right[0]) + (one(left[0], right[1]) + one(left[1], right[0]))


def turn(u, k0):
    angle = math.pi * u * (4 * k0 + 1) / 16
    return math.cos(angle), math.sin(angle)


def evaluate_kernel(
    first_far, second_far, keep_far, scale_far, high_far, low_far, twiddle_far,
    out,
    first, second, keep, scale, wide_high, wide_low, twiddle, held, sems,
):
    copies = [
        pltpu.make_async_copy(far, near, sems.at[place])
        for place, (far, near) in enumerate(
            (
                (first_far, first),
                (second_far, second),
                (twiddle_far, twiddle),
                (high_far, wide_high),
                (low_far, wide_low),
                (keep_far, keep),
                (scale_far, scale),
            )
        )
    ]
    for copy in copies:
        copy.start()
    copies[0].wait()
    copies[1].wait()
    for pair in range(2):
        for u in range(U):
            base = (pair * U + u) * 8
            for limb in range(2):
                for cipher, ref in enumerate((first, second)):
                    held[pl.ds(base + limb * 4 + cipher, 2, stride=2), :] = ref[
                        limb, pair, :, u * LANES : (u + 1) * LANES
                    ]
    copies[2].wait()
    copies[5].wait()
    copies[6].wait()
    lane = lax.broadcasted_iota(jnp.int32, (8, LANES), 1)
    table = jnp.zeros((8, LANES), f32)
    for i in range(16):
        for limb in range(2):
            place = limb * 16 + (i % 2) * 8 + i // 2
            table = jnp.where(lane == place, keep[limb, i], table)
            table = jnp.where(lane == 32 + place, scale[limb, i], table)
    for tile in range(ROOTS // 8):
        out[pl.ds(tile * 16 + 1, 8, stride=2), :] = table
    blocks = []
    for pair in range(2):
        parts = [held[(pair * U + u) * 8 : (pair * U + u + 1) * 8, :] for u in range(U)]
        spun = [None] * K0
        for k0 in range(K0 // 4):
            sums = []
            for start in range(4):
                real = imag = None
                for u in range(start, U, 4):
                    cosine, sine = turn(u, k0)
                    term_real = parts[u] if u == 0 else parts[u] * cosine
                    real = term_real if real is None else real + term_real
                    if u:
                        term_imag = parts[u] * sine
                        imag = term_imag if imag is None else imag + term_imag
                sums.append((real, imag))
            zero, one, two, three = sums
            even = (zero[0] + two[0], zero[1] + two[1])
            odd = (one[0] + three[0], one[1] + three[1])
            even_gap = (zero[0] - two[0], zero[1] - two[1])
            odd_gap = (three[1] - one[1], one[0] - three[0])
            spun[k0] = (even[0] + odd[0], even[1] + odd[1])
            spun[k0 + 2] = (even_gap[0] + odd_gap[0], even_gap[1] + odd_gap[1])
            spun[k0 + 4] = (even[0] - odd[0], even[1] - odd[1])
            spun[k0 + 6] = (even_gap[0] - odd_gap[0], even_gap[1] - odd_gap[1])
        reals, imags = [], []
        for k0 in range(K0):
            cosine = twiddle[k0 : k0 + 1, :]
            sine = twiddle[K0 + k0 : K0 + k0 + 1, :]
            real, imag = spun[k0]
            reals.append(real * cosine - imag * sine)
            imags.append(real * sine + imag * cosine)
        real = jnp.concatenate(reals, axis=0)
        imag = jnp.concatenate(imags, axis=0)
        blocks.append(jnp.concatenate([real, -imag], axis=1))
        blocks.append(jnp.concatenate([imag, real], axis=1))
    rows = jnp.concatenate(blocks, axis=0)
    copies[3].wait()
    copies[4].wait()
    left = jnp.concatenate([wide_high[...], wide_high[...], wide_low[...]], axis=1)
    halves = []
    for pair in range(2):
        high, low = split_value(jnp.concatenate(blocks[2 * pair : 2 * pair + 2], axis=0))
        halves.append(
            lax.dot_general(
                left, jnp.concatenate([high, low, high], axis=1), (((1,), (1,)), ((), ())), preferred_element_type=f32
            )
        )
    spectrum = jnp.concatenate(halves, axis=1)
    for pair in range(2):
        out[pl.ds(pair * 256, LANES, stride=2), :] = spectrum[:, pair * LANES : (pair + 1) * LANES]


def complex_scale(value, cosine, sine):
    real, imag = value
    if abs(cosine) < 1e-9:
        return (-imag, real) if sine > 0 else (imag, -real)
    if abs(abs(cosine) - abs(sine)) < 1e-9:
        if cosine * sine > 0:
            return (real - imag) * cosine, (real + imag) * cosine
        return (real + imag) * cosine, (imag - real) * cosine
    return real * cosine - imag * sine, real * sine + imag * cosine


def split_ring(values, theta):
    if len(values) == 1:
        return [(theta, values[0])]
    half = len(values) // 2
    cosine, sine = math.cos(theta / 2), math.sin(theta / 2)
    left, right = [], []
    for low, high in zip(values[:half], values[half:]):
        moved = complex_scale(high, cosine, sine)
        left.append((low[0] + moved[0], low[1] + moved[1]))
        right.append((low[0] - moved[0], low[1] - moved[1]))
    return split_ring(left, theta / 2) + split_ring(right, theta / 2 + math.pi)


def join_ring(values, theta):
    if len(values) == 1:
        return values
    half = len(values) // 2
    left = join_ring(values[:half], theta / 2)
    right = join_ring(values[half:], theta / 2 + math.pi)
    cosine, sine = math.cos(theta / 2), math.sin(theta / 2)
    low, high = [], []
    for one, two in zip(left, right):
        low.append((one[0] + two[0], one[1] + two[1]))
        high.append(complex_scale((one[0] - two[0], one[1] - two[1]), cosine, -sine))
    return low + high


def root_angles(count, theta):
    if count == 1:
        return [theta]
    return root_angles(count // 2, theta / 2) + root_angles(count // 2, theta / 2 + math.pi)


def mix(weights, values, dims):
    high, low = split_value(values)
    axis = dims[0][0]
    left = jnp.concatenate([weights[0], weights[0], weights[1]], axis=axis)
    return lax.dot_general(
        left, jnp.concatenate([high, low, high], axis=0), (dims, ((), ())), preferred_element_type=f32
    )


def tensor_kernel(spread, to_special, out):
    lane = lax.broadcasted_iota(jnp.int32, (8, LANES), 1)
    half = lane < 64
    sign = jnp.where(half, 1.0, -1.0).astype(f32)
    limb_low = (lane & 4) == 0
    comp = lax.broadcasted_iota(jnp.int32, (16, LANES), 1) & 3

    def roll(value, shift):
        return pltpu.roll(value, shift % LANES, 1)

    rows = jnp.concatenate([to_special[pl.ds(limb, 8, stride=2), :] for limb in range(2)], axis=0)
    old = lax.broadcasted_iota(jnp.int32, (16, 16), 0)
    new = lax.broadcasted_iota(jnp.int32, (16, 16), 1)
    order = jnp.where(old == 2 * (new & 7) + (new >> 3), 1.0, 0.0).astype(bf16)
    extend = split_value(
        sum(
            lax.dot_general(part, order, (((1,), (0,)), ((), ())), preferred_element_type=f32)
            for part in split_value(rows)
        )
    )
    table = spread[pl.ds(1, GROUPS, stride=2 * COEF), :]
    shrink = split_value(jnp.concatenate([table[:, 16 * j : 16 * j + 16] for j in range(4)], axis=0))

    blocks = [spread[pl.ds(2 * c, GROUPS, stride=2 * COEF), :] for c in range(COEF)]
    spectra = []
    for _, (real, imag) in split_ring(list(zip(blocks[: COEF // 2], blocks[COEF // 2 :])), math.pi / 2):
        one = real - roll(imag, 64)
        two = imag + roll(real, 64)
        spectra.append((jnp.where(half, one, two), jnp.where(half, two, one)))

    def tensor(value):
        real, imag = value
        real_next, imag_next = (jnp.where(comp == 3, roll(part, 3), roll(part, -1)) for part in value)
        return real * real_next - imag * imag_next, real * imag_next + imag * real_next

    owns = []
    for place in range(COEF // 4):
        for part in range(2):
            one, two = spectra[2 * place][part], spectra[2 * place + 1][part]
            owns.append(
                jnp.concatenate(
                    [jnp.where(limb_low, one, roll(two, 4)), jnp.where(limb_low, roll(one, -4), two)], axis=0
                )
            )
    specials = mix(extend, jnp.concatenate(owns, axis=1), ((1,), (0,)))
    own_products, special_products = [], []
    for place in range(COEF // 4):
        start = place * 2 * LANES
        own_products += tensor(owns[2 * place : 2 * place + 2])
        special_products += tensor(
            (specials[:, start : start + LANES], specials[:, start + LANES : start + 2 * LANES])
        )
    products = jnp.concatenate(
        [jnp.concatenate(own_products, axis=1), jnp.concatenate(special_products, axis=1)], axis=0
    )
    scaled = mix(shrink, products, ((0,), (0,)))
    mixed = []
    for place in range(COEF // 4):
        parts = []
        for part in range(2):
            start = (2 * place + part) * LANES
            low, high = scaled[:8, start : start + LANES], scaled[8:, start : start + LANES]
            parts.append((jnp.where(limb_low, low, roll(high, 4)), jnp.where(limb_low, roll(low, -4), high)))
        mixed.append((parts[0][0], parts[1][0]))
        mixed.append((parts[0][1], parts[1][1]))

    share = 1.0 / (COEF * BLOCK)
    joined = []
    for (real, imag), theta in zip(mixed, root_angles(COEF // 2, math.pi / 2)):
        cosine = share + sign * (share * math.sin(theta))
        sine = -share * math.cos(theta)
        own_real, own_imag = real * cosine - imag * sine, imag * cosine + real * sine
        other_real, other_imag = roll(own_real, 64), roll(own_imag, 64)
        joined.append(
            (
                jnp.where(half, own_real + other_real, own_imag + other_imag),
                jnp.where(half, own_imag - other_imag, own_real - other_real),
            )
        )
    for c, (real, imag) in enumerate(join_ring(joined, math.pi / 2)):
        out[pl.ds(c, GROUPS, stride=COEF), :] = real
        out[pl.ds(c + COEF // 2, GROUPS, stride=COEF), :] = imag


def restore_kernel(gathered, wide_high, wide_low, twiddle, out):
    row = lax.broadcasted_iota(jnp.int32, (8, LANES), 0)
    middle = (row & 3) == 1
    values = split_value(jnp.concatenate([gathered[:LANES, :], gathered[LANES:, :]], axis=1))
    left = jnp.concatenate([values[0], values[1], values[0]], axis=0)
    right = jnp.concatenate([wide_high[...], wide_high[...], wide_low[...]], axis=0)
    both = lax.dot_general(left, right, (((0,), (0,)), ((), ())), preferred_element_type=f32)
    for pair in range(2):
        spun = both[pair * LANES : (pair + 1) * LANES]
        real = spun[:64, :LANES] + spun[64:, LANES:]
        imag = spun[64:, :LANES] - spun[:64, LANES:]
        turned = []
        for k0 in range(K0):
            cosine = twiddle[k0 : k0 + 1, :]
            sine = twiddle[K0 + k0 : K0 + k0 + 1, :]
            own_real, own_imag = real[k0 * 8 : k0 * 8 + 8], imag[k0 * 8 : k0 * 8 + 8]
            turned.append((own_real * cosine + own_imag * sine, own_imag * cosine - own_real * sine))
        halves = []
        for k0 in range(K0 // 2):
            one, two = turned[k0], turned[k0 + K0 // 2]
            halves.append(((one[0] + two[0], one[1] + two[1]), (one[0] - two[0], one[1] - two[1])))
        quarters = []
        for k0 in range(K0 // 4):
            (even, odd), (even_far, odd_far) = halves[k0], halves[k0 + 2]
            quarters.append(
                (
                    (even[0] + even_far[0], even[1] + even_far[1]),
                    (odd[0] + odd_far[1], odd[1] - odd_far[0]),
                    (even[0] - even_far[0], even[1] - even_far[1]),
                    (odd[0] - odd_far[1], odd[1] + odd_far[0]),
                )
            )
        for u in range(U):
            total = None
            for k0 in range(K0 // 4):
                cosine, sine = turn(u, k0)
                real_part, imag_part = quarters[k0][u % 4]
                term = real_part if u == 0 else real_part * cosine + imag_part * sine
                total = term if total is None else total + term
            total = jnp.where(middle, total + pltpu.roll(total, 6, 0), total)
            for limb in range(2):
                for part in range(3):
                    row = limb * 4 + part
                    out[limb, part, pair : pair + 1, u * LANES : (u + 1) * LANES] = total[row : row + 1]


def in_vmem():
    return pl.BlockSpec(memory_space=pltpu.VMEM)


def in_hbm():
    return pl.BlockSpec(memory_space=pltpu.HBM)


def kept_far(*arrays):
    return [pltpu.with_memory_space_constraint(array, pltpu.HBM) for array in arrays]


def per_device(first_cipher, second_cipher, to_special, keep_table, scale_table):
    (wide_high, wide_low), twiddle = turn_tables()
    wide_high, wide_low, twiddle = jnp.asarray(wide_high), jnp.asarray(wide_low), jnp.asarray(twiddle)
    params = pltpu.CompilerParams(vmem_limit_bytes=32 * 1024 * 1024)
    spectra = pl.pallas_call(
        evaluate_kernel,
        out_shape=jax.ShapeDtypeStruct((2 * ROOTS, LANES), f32),
        in_specs=[in_hbm()] * 7,
        out_specs=in_vmem(),
        scratch_shapes=[
            pltpu.VMEM(first_cipher.shape, f32),
            pltpu.VMEM(second_cipher.shape, f32),
            pltpu.SMEM((2, 16), f32),
            pltpu.SMEM((2, 16), f32),
            pltpu.VMEM(wide_high.shape, bf16),
            pltpu.VMEM(wide_low.shape, bf16),
            pltpu.VMEM(twiddle.shape, f32),
            pltpu.VMEM((2 * U * 8 + 16, LANES), f32),
            pltpu.SemaphoreType.DMA((7,)),
        ],
        compiler_params=params,
        name="evaluate",
    )(*kept_far(first_cipher, second_cipher, keep_table.T, scale_table.T, wide_high, wide_low, twiddle))
    spread = lax.all_to_all(spectra.reshape(ROOTS, 1, 2 * LANES), ("limb", "coef"), 0, 0)
    scaled = pl.pallas_call(
        tensor_kernel,
        out_shape=jax.ShapeDtypeStruct((ROOTS, LANES), f32),
        in_specs=[in_vmem()] * 2,
        out_specs=in_vmem(),
        compiler_params=params,
        name="tensor",
    )(spread.reshape(2 * ROOTS, LANES), to_special)
    gathered = lax.all_to_all(scaled.reshape(ROOTS, 1, LANES), ("limb", "coef"), 0, 0)
    product = pl.pallas_call(
        restore_kernel,
        out_shape=jax.ShapeDtypeStruct((2, 3, 2, BLOCK), f32),
        in_specs=[in_vmem()] * 4,
        out_specs=in_vmem(),
        compiler_params=params,
        name="restore",
    )(gathered.reshape(ROOTS, LANES), wide_high, wide_low, twiddle)
    return product.transpose(0, 2, 1, 3)


def solution(mesh):
    return jax.shard_map(
        per_device,
        mesh=mesh,
        in_specs=(
            P("limb", None, None, "coef"),
            P("limb", None, None, "coef"),
            P(),
            P(None, "limb"),
            P(None, "limb"),
        ),
        out_specs=P("limb", None, None, "coef"),
        check_vma=False,
    )
```

```python
import math

import jax
import jax.numpy as jnp
import ml_dtypes
import numpy as np
from jax import lax
from jax.experimental import pallas as pl
from jax.experimental.pallas import tpu as pltpu
from jax.sharding import PartitionSpec as P

LANES = 128
U = 8
K0 = 8
BLOCK = U * LANES
COEF = 32
GROUPS = 8
ROOTS = 2 * LANES
f32 = jnp.float32
bf16 = jnp.bfloat16


def split_constant(values):
    high = values.astype(np.float32).astype(ml_dtypes.bfloat16)
    low = (values - high.astype(np.float64)).astype(ml_dtypes.bfloat16)
    return high, low


def turn_tables():
    index = np.arange(LANES)
    angle = 2 * np.pi * (index[:, None] * index[None, :] % LANES) / LANES
    wide = np.concatenate([np.cos(angle), np.sin(angle)], axis=1)
    v = np.arange(LANES)[None, :]
    k0 = np.arange(K0)[:, None]
    phase = np.pi * v * (4 * k0 + 1) / 2048
    twiddle = np.concatenate([np.cos(phase), np.sin(phase)], axis=0)
    return split_constant(wide), twiddle.astype(np.float32)


def split_value(values):
    high = values.astype(bf16)
    low = (values - high.astype(f32)).astype(bf16)
    return high, low


def dot3(left, right, dims):
    def one(a, b):
        return lax.dot_general(a, b, (dims, ((), ())), preferred_element_type=f32)

    return one(left[0], right[0]) + (one(left[0], right[1]) + one(left[1], right[0]))


def turn(u, k0):
    angle = math.pi * u * (4 * k0 + 1) / 16
    return math.cos(angle), math.sin(angle)


def evaluate_kernel(
    first_far, second_far, keep_far, scale_far, high_far, low_far, twiddle_far,
    out,
    first, second, keep, scale, wide_high, wide_low, twiddle, held, sems,
):
    copies = [
        pltpu.make_async_copy(far, near, sems.at[place])
        for place, (far, near) in enumerate(
            (
                (first_far, first),
                (second_far, second),
                (twiddle_far, twiddle),
                (high_far, wide_high),
                (low_far, wide_low),
                (keep_far, keep),
                (scale_far, scale),
            )
        )
    ]
    for copy in copies:
        copy.start()
    copies[0].wait()
    copies[1].wait()
    for pair in range(2):
        for u in range(U):
            base = (pair * U + u) * 8
            for limb in range(2):
                for cipher, ref in enumerate((first, second)):
                    held[pl.ds(base + limb * 4 + cipher, 2, stride=2), :] = ref[
                        limb, pair, :, u * LANES : (u + 1) * LANES
                    ]
    copies[2].wait()
    copies[5].wait()
    copies[6].wait()
    lane = lax.broadcasted_iota(jnp.int32, (8, LANES), 1)
    table = jnp.zeros((8, LANES), f32)
    for i in range(16):
        for limb in range(2):
            place = limb * 16 + (i % 2) * 8 + i // 2
            table = jnp.where(lane == place, keep[limb, i], table)
            table = jnp.where(lane == 32 + place, scale[limb, i], table)
    for tile in range(ROOTS // 8):
        out[pl.ds(tile * 16 + 1, 8, stride=2), :] = table
    blocks = []
    for pair in range(2):
        parts = [held[(pair * U + u) * 8 : (pair * U + u + 1) * 8, :] for u in range(U)]
        spun = [None] * K0
        for k0 in range(K0 // 4):
            sums = []
            for start in range(4):
                real = imag = None
                for u in range(start, U, 4):
                    cosine, sine = turn(u, k0)
                    term_real = parts[u] if u == 0 else parts[u] * cosine
                    real = term_real if real is None else real + term_real
                    if u:
                        term_imag = parts[u] * sine
                        imag = term_imag if imag is None else imag + term_imag
                sums.append((real, imag))
            zero, one, two, three = sums
            even = (zero[0] + two[0], zero[1] + two[1])
            odd = (one[0] + three[0], one[1] + three[1])
            even_gap = (zero[0] - two[0], zero[1] - two[1])
            odd_gap = (three[1] - one[1], one[0] - three[0])
            spun[k0] = (even[0] + odd[0], even[1] + odd[1])
            spun[k0 + 2] = (even_gap[0] + odd_gap[0], even_gap[1] + odd_gap[1])
            spun[k0 + 4] = (even[0] - odd[0], even[1] - odd[1])
            spun[k0 + 6] = (even_gap[0] - odd_gap[0], even_gap[1] - odd_gap[1])
        reals, imags = [], []
        for k0 in range(K0):
            cosine = twiddle[k0 : k0 + 1, :]
            sine = twiddle[K0 + k0 : K0 + k0 + 1, :]
            real, imag = spun[k0]
            reals.append(real * cosine - imag * sine)
            imags.append(real * sine + imag * cosine)
        real = jnp.concatenate(reals, axis=0)
        imag = jnp.concatenate(imags, axis=0)
        blocks.append(jnp.concatenate([real, -imag], axis=1))
        blocks.append(jnp.concatenate([imag, real], axis=1))
    rows = jnp.concatenate(blocks, axis=0)
    copies[3].wait()
    copies[4].wait()
    left = jnp.concatenate([wide_high[...], wide_high[...], wide_low[...]], axis=1)
    halves = []
    for pair in range(2):
        high, low = split_value(jnp.concatenate(blocks[2 * pair : 2 * pair + 2], axis=0))
        halves.append(
            lax.dot_general(
                left, jnp.concatenate([high, low, high], axis=1), (((1,), (1,)), ((), ())), preferred_element_type=f32
            )
        )
    spectrum = jnp.concatenate(halves, axis=1)
    for pair in range(2):
        out[pl.ds(pair * 256, LANES, stride=2), :] = spectrum[:, pair * LANES : (pair + 1) * LANES]


def complex_scale(value, cosine, sine):
    real, imag = value
    if abs(cosine) < 1e-9:
        return (-imag, real) if sine > 0 else (imag, -real)
    if abs(abs(cosine) - abs(sine)) < 1e-9:
        if cosine * sine > 0:
            return (real - imag) * cosine, (real + imag) * cosine
        return (real + imag) * cosine, (imag - real) * cosine
    return real * cosine - imag * sine, real * sine + imag * cosine


def split_ring(values, theta):
    if len(values) == 1:
        return [(theta, values[0])]
    half = len(values) // 2
    cosine, sine = math.cos(theta / 2), math.sin(theta / 2)
    left, right = [], []
    for low, high in zip(values[:half], values[half:]):
        moved = complex_scale(high, cosine, sine)
        left.append((low[0] + moved[0], low[1] + moved[1]))
        right.append((low[0] - moved[0], low[1] - moved[1]))
    return split_ring(left, theta / 2) + split_ring(right, theta / 2 + math.pi)


def join_ring(values, theta):
    if len(values) == 1:
        return values
    half = len(values) // 2
    left = join_ring(values[:half], theta / 2)
    right = join_ring(values[half:], theta / 2 + math.pi)
    cosine, sine = math.cos(theta / 2), math.sin(theta / 2)
    low, high = [], []
    for one, two in zip(left, right):
        low.append((one[0] + two[0], one[1] + two[1]))
        high.append(complex_scale((one[0] - two[0], one[1] - two[1]), cosine, -sine))
    return low + high


def root_angles(count, theta):
    if count == 1:
        return [theta]
    return root_angles(count // 2, theta / 2) + root_angles(count // 2, theta / 2 + math.pi)


def mix(weights, values, dims):
    high, low = split_value(values)
    axis = dims[0][0]
    left = jnp.concatenate([weights[0], weights[0], weights[1]], axis=axis)
    return lax.dot_general(
        left, jnp.concatenate([high, low, high], axis=0), (dims, ((), ())), preferred_element_type=f32
    )


def tensor_kernel(spread, to_special, out):
    lane = lax.broadcasted_iota(jnp.int32, (8, LANES), 1)
    half = lane < 64
    sign = jnp.where(half, 1.0, -1.0).astype(f32)
    limb_low = (lane & 4) == 0
    comp = lax.broadcasted_iota(jnp.int32, (16, LANES), 1) & 3

    def roll(value, shift):
        return pltpu.roll(value, shift % LANES, 1)

    rows = jnp.concatenate([to_special[pl.ds(limb, 8, stride=2), :] for limb in range(2)], axis=0)
    old = lax.broadcasted_iota(jnp.int32, (16, 16), 0)
    new = lax.broadcasted_iota(jnp.int32, (16, 16), 1)
    order = jnp.where(old == 2 * (new & 7) + (new >> 3), 1.0, 0.0).astype(bf16)
    extend = split_value(
        sum(
            lax.dot_general(part, order, (((1,), (0,)), ((), ())), preferred_element_type=f32)
            for part in split_value(rows)
        )
    )
    table = spread[pl.ds(1, GROUPS, stride=2 * COEF), :]
    shrink = split_value(jnp.concatenate([table[:, 16 * j : 16 * j + 16] for j in range(4)], axis=0))

    blocks = [spread[pl.ds(2 * c, GROUPS, stride=2 * COEF), :] for c in range(COEF)]
    spectra = []
    for _, (real, imag) in split_ring(list(zip(blocks[: COEF // 2], blocks[COEF // 2 :])), math.pi / 2):
        one = real - roll(imag, 64)
        two = imag + roll(real, 64)
        spectra.append((jnp.where(half, one, two), jnp.where(half, two, one)))

    def tensor(value):
        real, imag = value
        real_next, imag_next = (jnp.where(comp == 3, roll(part, 3), roll(part, -1)) for part in value)
        return real * real_next - imag * imag_next, real * imag_next + imag * real_next

    owns = []
    for place in range(COEF // 4):
        for part in range(2):
            one, two = spectra[2 * place][part], spectra[2 * place + 1][part]
            owns.append(
                jnp.concatenate(
                    [jnp.where(limb_low, one, roll(two, 4)), jnp.where(limb_low, roll(one, -4), two)], axis=0
                )
            )
    specials = mix(extend, jnp.concatenate(owns, axis=1), ((1,), (0,)))
    own_products, special_products = [], []
    for place in range(COEF // 4):
        start = place * 2 * LANES
        own_products += tensor(owns[2 * place : 2 * place + 2])
        special_products += tensor(
            (specials[:, start : start + LANES], specials[:, start + LANES : start + 2 * LANES])
        )
    products = jnp.concatenate(
        [jnp.concatenate(own_products, axis=1), jnp.concatenate(special_products, axis=1)], axis=0
    )
    scaled = mix(shrink, products, ((0,), (0,)))
    mixed = []
    for place in range(COEF // 4):
        parts = []
        for part in range(2):
            start = (2 * place + part) * LANES
            low, high = scaled[:8, start : start + LANES], scaled[8:, start : start + LANES]
            parts.append((jnp.where(limb_low, low, roll(high, 4)), jnp.where(limb_low, roll(low, -4), high)))
        mixed.append((parts[0][0], parts[1][0]))
        mixed.append((parts[0][1], parts[1][1]))

    share = 1.0 / (COEF * BLOCK)
    joined = []
    for (real, imag), theta in zip(mixed, root_angles(COEF // 2, math.pi / 2)):
        cosine = share + sign * (share * math.sin(theta))
        sine = -share * math.cos(theta)
        own_real, own_imag = real * cosine - imag * sine, imag * cosine + real * sine
        other_real, other_imag = roll(own_real, 64), roll(own_imag, 64)
        joined.append(
            (
                jnp.where(half, own_real + other_real, own_imag + other_imag),
                jnp.where(half, own_imag - other_imag, own_real - other_real),
            )
        )
    for c, (real, imag) in enumerate(join_ring(joined, math.pi / 2)):
        out[pl.ds(c, GROUPS, stride=COEF), :] = real
        out[pl.ds(c + COEF // 2, GROUPS, stride=COEF), :] = imag


def restore_kernel(gathered, wide_high, wide_low, twiddle, out):
    row = lax.broadcasted_iota(jnp.int32, (8, LANES), 0)
    middle = (row & 3) == 1
    values = split_value(jnp.concatenate([gathered[:LANES, :], gathered[LANES:, :]], axis=1))
    left = jnp.concatenate([values[0], values[1], values[0]], axis=0)
    right = jnp.concatenate([wide_high[...], wide_high[...], wide_low[...]], axis=0)
    both = lax.dot_general(left, right, (((0,), (0,)), ((), ())), preferred_element_type=f32)
    for pair in range(2):
        spun = both[pair * LANES : (pair + 1) * LANES]
        real = spun[:64, :LANES] + spun[64:, LANES:]
        imag = spun[64:, :LANES] - spun[:64, LANES:]
        turned = []
        for k0 in range(K0):
            cosine = twiddle[k0 : k0 + 1, :]
            sine = twiddle[K0 + k0 : K0 + k0 + 1, :]
            own_real, own_imag = real[k0 * 8 : k0 * 8 + 8], imag[k0 * 8 : k0 * 8 + 8]
            turned.append((own_real * cosine + own_imag * sine, own_imag * cosine - own_real * sine))
        halves = []
        for k0 in range(K0 // 2):
            one, two = turned[k0], turned[k0 + K0 // 2]
            halves.append(((one[0] + two[0], one[1] + two[1]), (one[0] - two[0], one[1] - two[1])))
        for u in range(U):
            total = None
            for k0 in range(K0 // 2):
                cosine, sine = turn(u, k0)
                real_part, imag_part = halves[k0][u % 2]
                term = real_part if u == 0 else real_part * cosine + imag_part * sine
                total = term if total is None else total + term
            total = jnp.where(middle, total + pltpu.roll(total, 6, 0), total)
            for limb in range(2):
                for part in range(3):
                    row = limb * 4 + part
                    out[limb, part, pair : pair + 1, u * LANES : (u + 1) * LANES] = total[row : row + 1]


def in_vmem():
    return pl.BlockSpec(memory_space=pltpu.VMEM)


def in_hbm():
    return pl.BlockSpec(memory_space=pltpu.HBM)


def kept_far(*arrays):
    return [pltpu.with_memory_space_constraint(array, pltpu.HBM) for array in arrays]


def per_device(first_cipher, second_cipher, to_special, keep_table, scale_table):
    (wide_high, wide_low), twiddle = turn_tables()
    wide_high, wide_low, twiddle = jnp.asarray(wide_high), jnp.asarray(wide_low), jnp.asarray(twiddle)
    params = pltpu.CompilerParams(vmem_limit_bytes=32 * 1024 * 1024)
    spectra = pl.pallas_call(
        evaluate_kernel,
        out_shape=jax.ShapeDtypeStruct((2 * ROOTS, LANES), f32),
        in_specs=[in_hbm()] * 7,
        out_specs=in_vmem(),
        scratch_shapes=[
            pltpu.VMEM(first_cipher.shape, f32),
            pltpu.VMEM(second_cipher.shape, f32),
            pltpu.SMEM((2, 16), f32),
            pltpu.SMEM((2, 16), f32),
            pltpu.VMEM(wide_high.shape, bf16),
            pltpu.VMEM(wide_low.shape, bf16),
            pltpu.VMEM(twiddle.shape, f32),
            pltpu.VMEM((2 * U * 8 + 16, LANES), f32),
            pltpu.SemaphoreType.DMA((7,)),
        ],
        compiler_params=params,
        name="evaluate",
    )(*kept_far(first_cipher, second_cipher, keep_table.T, scale_table.T, wide_high, wide_low, twiddle))
    spread = lax.all_to_all(spectra.reshape(ROOTS, 2, LANES), ("limb", "coef"), 0, 0)
    scaled = pl.pallas_call(
        tensor_kernel,
        out_shape=jax.ShapeDtypeStruct((ROOTS, LANES), f32),
        in_specs=[in_vmem()] * 2,
        out_specs=in_vmem(),
        compiler_params=params,
        name="tensor",
    )(spread.reshape(2 * ROOTS, LANES), to_special)
    gathered = lax.all_to_all(scaled.reshape(ROOTS, 1, LANES), ("limb", "coef"), 0, 0)
    product = pl.pallas_call(
        restore_kernel,
        out_shape=jax.ShapeDtypeStruct((2, 3, 2, BLOCK), f32),
        in_specs=[in_vmem()] * 4,
        out_specs=in_vmem(),
        compiler_params=params,
        name="restore",
    )(gathered.reshape(ROOTS, LANES), wide_high, wide_low, twiddle)
    return product.transpose(0, 2, 1, 3)


def solution(mesh):
    return jax.shard_map(
        per_device,
        mesh=mesh,
        in_specs=(
            P("limb", None, None, "coef"),
            P("limb", None, None, "coef"),
            P(),
            P(None, "limb"),
            P(None, "limb"),
        ),
        out_specs=P("limb", None, None, "coef"),
        check_vma=False,
    )
```
